128 devices in a mesh: blk: 32 (over y, z, core), span: 4 (over x).
Axes of the slice: x: 4, y: 4, z: 4, core: 2. Of those that a mesh axis runs over, the one named last changes fastest.
Arguments:
- disp: float32 [3, 24, 64, 4096], P(None, None, 'span', 'blk'), may hold values from -6 to 6
- velocity: float32 [3, 24, 64, 4096], P(None, None, 'span', 'blk'), may hold values from -3 to 3
- modulus: float32 [24, 64, 4096], P(None, 'span', 'blk'), may hold values from 0.5 to 4
- guess_circ: float32 [32, 2, 6, 3, 24, 64], P('blk', None, None, None, None, 'span'), may hold values from -6 to 6
- guess_height: float32 [4, 2, 6, 3, 24, 4096], P('span', None, None, None, None, 'blk'), may hold values from -6 to 6
- pair_match: int32 [32, 4, 384], P('blk', 'span'), may hold values from 0 to 383, each once within a row
- patch_owner: int32 [32, 4, 384], P('blk', 'span'), may hold values from 0 to 4095
Outputs:
- disp_end: float32 [3, 24, 64, 4096], P(None, None, 'span', 'blk')
- circ_next: float32 [32, 2, 6, 3, 24, 64], P('blk', None, None, None, None, 'span')
- height_next: float32 [4, 2, 6, 3, 24, 4096], P('span', None, None, None, None, 'blk')
- patch_load: float32 [3, 4096], P(None, ('blk', 'span'))
The draws below stay inside these ranges and needn't reach their ends.
Inputs may be any that keep to these rules, and one draw needn't show every extreme that they name: `pair_match`: each device's block of 384 entries is a permutation.
All inputs are finite; a program needn't handle non-finite values.
Results may differ from the reference program's by a relative error of at most 0.0003.
Values sent between devices are 32-bit elements; how exact they have to be, the bound alone decides.
No kernel may reach another device: no remote copies, remote signals or barrier semaphores. Data moves between devices by JAX's collectives and lax.ppermute only.
A program may use at most 128 MiB of HBM per device.

```python
import math
import jax
import jax.numpy as jnp
from jax import lax

THICK = 24
HEIGHT = 16
ARC = 128
STEPS = 6
HEIGHT_ALL = 64
ARC_ALL = 4096
PATCHES = 4096
N_BLK = 32
N_SPAN = 4


def touch_ends(entries, stream_key, low, high):
    spot = [jax.random.randint(jax.random.fold_in(stream_key, axis), (), 0, length) for axis, length in enumerate(entries.shape)]
    widest = entries.shape.index(max(entries.shape))
    beside = spot[:widest] + [(spot[widest] + 1) % entries.shape[widest]] + spot[widest + 1:]
    return entries.at[tuple(spot)].set(low).at[tuple(beside)].set(high)


def level_of(own_key, extent, split, smallest, top_value):
    level, own = 1.0, jax.random.fold_in(own_key, 6)
    for dim, shards_of in split:
        draws = jnp.exp(jax.random.uniform(jax.random.fold_in(own, dim), (shards_of,), jnp.float32, smallest / len(split), top_value / len(split)))
        level = level * jnp.repeat(draws, extent[dim] // shards_of).reshape([-1 if axis == dim else 1 for axis in range(len(extent))])
    return level


def bell_draw(rng, shape, spread, limit, pieces=(), kind=jnp.bfloat16):
    level = level_of(rng, shape, pieces, -0.22, 0.18) if pieces else 1.0
    values = jax.random.normal(rng, shape, jnp.float32) * spread * level
    return jnp.minimum(jnp.maximum(values, -limit), limit).astype(kind)


def setup_inputs(seed: int = 0) -> dict:
    streams_of = jax.random.split(jax.random.key(seed), 8)
    return {
        "disp": bell_draw(streams_of[0], (3, THICK, HEIGHT_ALL, ARC_ALL), 1.0, 6.0, ((2, 4), (3, 32)), jnp.float32),
        "velocity": bell_draw(streams_of[1], (3, THICK, HEIGHT_ALL, ARC_ALL), 0.5, 3.0, ((2, 4), (3, 32)), jnp.float32),
        "modulus": jnp.clip(jnp.exp(math.log(4.0) - 2.0794415 * jax.random.uniform(streams_of[2], (THICK, HEIGHT_ALL, ARC_ALL), jnp.float32) ** level_of(streams_of[2], (THICK, HEIGHT_ALL, ARC_ALL), ((1, 4), (2, 32)), -0.2, 0.2)), 0.5, 4.0),
        "guess_circ": bell_draw(streams_of[3], (N_BLK, 2, STEPS, 3, THICK, HEIGHT_ALL), 1.0, 6.0, ((0, 32), (5, 4)), jnp.float32),
        "guess_height": bell_draw(streams_of[4], (N_SPAN, 2, STEPS, 3, THICK, ARC_ALL), 1.0, 6.0, ((0, 4), (5, 32)), jnp.float32),
        "pair_match": jax.vmap(lambda own: jax.random.permutation(own, THICK * HEIGHT))(jax.random.split(streams_of[5], N_BLK * N_SPAN)).reshape((N_BLK, N_SPAN, THICK * HEIGHT)).astype(jnp.int32),
        "patch_owner": touch_ends(jax.random.randint(streams_of[6], (N_BLK, N_SPAN, THICK * HEIGHT), 0, PATCHES), jax.random.fold_in(streams_of[6], 1), 0, PATCHES - 1).astype(jnp.int32),
    }


time_step = 0.2

def interior(current, faces):
    along_k, along_h, along_a = faces
    diff = along_k * (current[:, 1:] - current[:, :-1])
    total = jnp.pad(diff, ((0, 0), (0, 1), (0, 0), (0, 0))) - jnp.pad(diff, ((0, 0), (1, 0), (0, 0), (0, 0)))
    diff = along_h * (current[:, :, 1:] - current[:, :, :-1])
    total = total + jnp.pad(diff, ((0, 0), (0, 0), (0, 1), (0, 0))) - jnp.pad(diff, ((0, 0), (0, 0), (1, 0), (0, 0)))
    diff = along_a * (current[:, :, :, 1:] - current[:, :, :, :-1])
    total = total + jnp.pad(diff, ((0, 0), (0, 0), (0, 0), (0, 1))) - jnp.pad(diff, ((0, 0), (0, 0), (0, 0), (1, 0)))
    return total

def subdomain(start, speed, moduli, g_west, g_east, g_south, g_north):
    faces = (0.5 * (moduli[1:] + moduli[:-1]), 0.5 * (moduli[:, 1:] + moduli[:, :-1]), 0.5 * (moduli[:, :, 1:] + moduli[:, :, :-1]))
    imp_west = jnp.sqrt(moduli[:, :, 0])
    imp_east = jnp.sqrt(moduli[:, :, -1])
    imp_south = jnp.sqrt(moduli[:, 0, :])
    imp_north = jnp.sqrt(moduli[:, -1, :])
    older = start - time_step * speed
    current = start
    records = [[], [], [], [], [], [], [], []]
    for step in range(STEPS):
        rate_w = imp_west * ((current[:, :, :, 0] - older[:, :, :, 0]) / time_step)
        rate_e = imp_east * ((current[:, :, :, -1] - older[:, :, :, -1]) / time_step)
        rate_s = imp_south * ((current[:, :, 0, :] - older[:, :, 0, :]) / time_step)
        rate_n = imp_north * ((current[:, :, -1, :] - older[:, :, -1, :]) / time_step)
        phi_w = g_west[step] - rate_w
        phi_e = g_east[step] - rate_e
        phi_s = g_south[step] - rate_s
        phi_n = g_north[step] - rate_n
        total = interior(current, faces)
        total = total.at[:, :, :, 0].add(phi_w).at[:, :, :, -1].add(phi_e)
        total = total.at[:, :, 0, :].add(phi_s).at[:, :, -1, :].add(phi_n)
        following = 2.0 * current - older + time_step * time_step * total
        older, current = (current, following)
        for slot, value in enumerate((phi_w, rate_w, phi_e, rate_e, phi_s, rate_s, phi_n, rate_n)):
            records[slot].append(value)
    stacked = [jnp.stack(item) for item in records]
    load = lax.optimization_barrier(jnp.sum(stacked[2], axis=0))
    return (current,) + tuple(stacked) + (load,)

def sweep_all(disp, velocity, modulus, g_west, g_east, g_south, g_north):

    def one(index):
        row = index // N_BLK
        col = index % N_BLK
        zero = jnp.int32(0)
        start_h = (row * HEIGHT).astype(jnp.int32)
        start_a = (col * ARC).astype(jnp.int32)
        block = lax.dynamic_slice(disp, (zero, zero, start_h, start_a), (3, THICK, HEIGHT, ARC))
        speed = lax.dynamic_slice(velocity, (zero, zero, start_h, start_a), (3, THICK, HEIGHT, ARC))
        moduli = lax.dynamic_slice(modulus, (zero, start_h, start_a), (THICK, HEIGHT, ARC))
        return subdomain(block, speed, moduli, g_west[row, col], g_east[row, col], g_south[row, col], g_north[row, col])
    results = lax.map(one, jnp.arange(N_SPAN * N_BLK, dtype=jnp.int32))
    return tuple((item.reshape((N_SPAN, N_BLK) + item.shape[1:]) for item in results))

def route(results, pair_match):
    final, phi_w, rate_w, phi_e, rate_e, phi_s, rate_s, phi_n, rate_n, load = results
    flat = THICK * HEIGHT
    send_w = (rate_w - phi_w).reshape(N_SPAN, N_BLK, STEPS, 3, flat)
    send_e = (rate_e - phi_e).reshape(N_SPAN, N_BLK, STEPS, 3, flat)
    send_s = rate_s - phi_s
    send_n = rate_n - phi_n
    match_t = pair_match.transpose(1, 0, 2)
    match = jnp.broadcast_to(match_t[:, :, None, None, :], send_w.shape)
    new_w = jnp.take_along_axis(jnp.roll(send_e, 1, axis=1), match, axis=4)
    span_ids = jnp.arange(N_SPAN, dtype=jnp.int32)[:, None, None]
    blk_ids = jnp.arange(N_BLK, dtype=jnp.int32)[None, :, None]
    iota = jnp.broadcast_to(jnp.arange(flat, dtype=jnp.int32)[None, None, :], match_t.shape)
    inverse = jnp.zeros_like(match_t).at[span_ids, blk_ids, match_t].set(iota)
    inverse = jnp.broadcast_to(inverse[:, :, None, None, :], send_w.shape)
    placed = jnp.take_along_axis(send_w, inverse, axis=4)
    new_e = jnp.roll(placed, -1, axis=1)
    new_s = jnp.concatenate([jnp.zeros_like(send_n[:1]), send_n[:-1]], axis=0)
    new_n = jnp.concatenate([send_s[1:], jnp.zeros_like(send_s[:1])], axis=0)
    shape = (N_SPAN, N_BLK, STEPS, 3, THICK, HEIGHT)
    return (new_w.reshape(shape), new_e.reshape(shape), new_s, new_n)

def reference(disp, velocity, modulus, guess_circ, guess_height, pair_match, patch_owner):
    circ = guess_circ.reshape(N_BLK, 2, STEPS, 3, THICK, N_SPAN, HEIGHT).transpose(5, 0, 1, 2, 3, 4, 6)
    rising = guess_height.reshape(N_SPAN, 2, STEPS, 3, THICK, N_BLK, ARC).transpose(0, 5, 1, 2, 3, 4, 6)
    data = (circ[:, :, 0], circ[:, :, 1], rising[:, :, 0], rising[:, :, 1])
    for sweep in range(2):
        results = sweep_all(disp, velocity, modulus, *data)
        data = route(results, pair_match)
    final = results[0].transpose(2, 3, 0, 4, 1, 5).reshape(3, THICK, N_SPAN * HEIGHT, N_BLK * ARC)
    load = results[9].reshape(N_SPAN * N_BLK, 3, THICK * HEIGHT).transpose(0, 2, 1).reshape(-1, 3)
    owners = patch_owner.transpose(1, 0, 2).reshape(-1)
    patch_load = jax.ops.segment_sum(load, owners, num_segments=PATCHES).T
    circ_next = jnp.stack([data[0], data[1]], axis=2).transpose(1, 2, 3, 4, 5, 0, 6).reshape(N_BLK, 2, STEPS, 3, THICK, N_SPAN * HEIGHT)
    height_next = jnp.stack([data[2], data[3]], axis=2).transpose(0, 2, 3, 4, 5, 1, 6).reshape(N_SPAN, 2, STEPS, 3, THICK, N_BLK * ARC)
    return (final, circ_next, height_next, patch_load)
```

```python
import jax
import jax.numpy as jnp
from jax import lax
from jax.experimental import pallas as pl
from jax.experimental.pallas import tpu as pltpu
from jax.sharding import PartitionSpec as P

STEPS = 6
COMPS = 3
THICK = 24
HEIGHT = 16
ARC = 128
FLAT = THICK * HEIGHT
LAYERS = 3
FACE_ROWS = STEPS * COMPS * THICK
PAD_ROWS = 8 * COMPS * THICK
LOAD_ROW = STEPS * COMPS
PATCH_DEV = 32
DEVICES = 128


def roll(values, shift, axis):
    shift %= values.shape[axis]
    return values if shift == 0 else pltpu.roll(values, shift, axis)


def iota(shape, axis):
    return lax.broadcasted_iota(jnp.int32, shape, axis)


def thickness_rows(first, layer, stride=1):
    return pl.ds(first + layer * stride, 8, stride=LAYERS * stride)


def prepare(disp, velocity, modulus, w):
    lane = iota((8, ARC), 1)
    sub = iota((8, ARC), 0)
    zero = jnp.zeros((8, ARC), jnp.float32)
    moduli = [
        roll(modulus[thickness_rows(0, l, HEIGHT), :], 0, 1) for l in range(LAYERS)
    ]
    west = [zero] * LAYERS
    east = [zero] * LAYERS
    for h in range(HEIGHT):
        on_west = lane == h
        on_east = lane == (h - 1) % ARC
        if h + 1 < HEIGHT:
            above = [
                roll(modulus[thickness_rows(h + 1, l, HEIGHT), :], h + 1, 1) for l in range(LAYERS)
            ]
        for l in range(LAYERS):
            m = moduli[l]
            w["along_a"][h, l] = jnp.where(on_east, 0.0, 0.02 * (m + roll(m, -1, 1)))
            if l + 1 < LAYERS:
                w["along_k"][h, l] = 0.02 * (m + moduli[l + 1])
            else:
                w["along_k"][h, l] = jnp.where(sub == 7, 0.0, 0.02 * (m + roll(moduli[0], -1, 0)))
            if h + 1 < HEIGHT:
                w["along_h"][h, l] = 0.02 * (m + roll(above[l], -1, 1))
            imp = jnp.sqrt(m)
            damp = jnp.where(on_west | on_east, imp, 0.0)
            if h == 0:
                damp = damp + imp
                w["faces"][2, l] = 5.0 * imp
            if h == HEIGHT - 1:
                damp = damp + imp
                w["faces"][3, l] = 5.0 * imp
            w["keep"][h, l] = 1.0 - 0.2 * damp
            west[l] = jnp.where(on_west, 5.0 * imp, west[l])
            east[l] = jnp.where(on_east, 5.0 * imp, east[l])
        for c in range(COMPS):
            for l in range(LAYERS):
                rows = thickness_rows(c * THICK * HEIGHT + h, l, HEIGHT)
                w["cur"][h, c * LAYERS + l] = roll(disp[rows, :], h, 1)
                w["vel"][h, c * LAYERS + l] = roll(0.2 * velocity[rows, :], h, 1)
        if h + 1 < HEIGHT:
            moduli = above
    for l in range(LAYERS):
        w["faces"][0, l] = west[l]
        w["faces"][1, l] = east[l]


def record(step, data, sends, w):
    south, south_at, north, north_at = data
    send_south, send_north = sends
    lane = iota((8, ARC), 1)
    zero = jnp.zeros((8, ARC), jnp.float32)
    for c in range(COMPS):
        for l in range(LAYERS):
            b = c * LAYERS + l
            west, east = zero, zero
            for h in range(HEIGHT):
                v = w["vel"][h, b]
                west = jnp.where(lane == h, v, west)
                east = jnp.where(lane == (h - 1) % ARC, v, east)
            rows = thickness_rows(step * (COMPS * THICK) + c * THICK, l)
            g = w["g_west"][rows, :]
            w["inject"][0, b] = 0.04 * g
            w["send_west"][rows, :] = 2.0 * (w["faces"][0, l] * west) - g
            g = w["g_east"][rows, :]
            w["inject"][1, b] = 0.04 * g
            rate = w["faces"][1, l] * east
            w["send_east"][rows, :] = 2.0 * rate - g
            w["load"][b] = w["load"][b] + (g - rate)
            at = thickness_rows(south_at + step * (COMPS * THICK) + c * THICK, l)
            g = south[at, :]
            w["inject"][2, b] = 0.04 * g
            send_south[rows, :] = 2.0 * (w["faces"][2, l] * w["vel"][0, b]) - g
            at = thickness_rows(north_at + step * (COMPS * THICK) + c * THICK, l)
            g = north[at, :]
            w["inject"][3, b] = roll(0.04 * g, HEIGHT - 1, 1)
            rate = w["faces"][3, l] * w["vel"][HEIGHT - 1, b]
            send_north[rows, :] = roll(2.0 * rate, 1 - HEIGHT, 1) - g


def update(w):
    lane = iota((8, ARC), 1)
    blocks = [(c, l) for c in range(COMPS) for l in range(LAYERS)]
    cur = {b: w["cur"][0, b[0] * LAYERS + b[1]] for b in blocks}
    left = {b: roll(cur[b], -1, 1) for b in blocks}
    rising = {}
    for h in range(HEIGHT):
        on_west = lane == h
        on_edge = on_west | (lane == (h - 1) % ARC)
        last = h + 1 == HEIGHT
        cur_next, left_next = {}, {}
        for c in range(COMPS):
            flux_k = []
            for l in range(LAYERS):
                here = cur[c, l]
                over = cur[c, l + 1] if l + 1 < LAYERS else roll(cur[c, 0], -1, 0)
                flux_k.append(w["along_k"][h, l] * (over - here))
            for l in range(LAYERS):
                b = (c, l)
                at = c * LAYERS + l
                here = cur[b]
                flux_a = w["along_a"][h, l] * (left[b] - here)
                total = flux_k[l] - (flux_k[l - 1] if l else roll(flux_k[LAYERS - 1], 1, 0))
                back = flux_a
                if h:
                    back = back + rising[b]
                total = total + flux_a - roll(back, 1, 1)
                if not last:
                    cur_next[b] = w["cur"][h + 1, at]
                    left_next[b] = roll(cur_next[b], -1, 1)
                    rising[b] = w["along_h"][h, l] * (left_next[b] - here)
                    total = total + rising[b]
                g = jnp.where(on_west, w["inject"][0, at], w["inject"][1, at])
                total = total + jnp.where(on_edge, g, 0.0)
                if h == 0:
                    total = total + w["inject"][2, at]
                if last:
                    total = total + w["inject"][3, at]
                v = w["keep"][h, l] * w["vel"][h, at] + total
                w["vel"][h, at] = v
                w["cur"][h, at] = here + v
        cur, left = cur_next, left_next


def gather_rows(history, offset):
    lane = iota((24, ARC), 1)
    parts = []
    for v in range(3):
        part = None
        for t in range(8):
            rows = roll(history[pl.ds(8 * v + t, 24, stride=THICK), :], HEIGHT * t - offset, 1)
            part = rows if part is None else jnp.where(lane >= HEIGHT * t, rows, part)
        parts.append(part)
    return jnp.concatenate(parts, axis=1)


def scatter_rows(flat, history, offset):
    for v in range(3):
        part = flat[:, v * ARC : (v + 1) * ARC]
        for t in range(8):
            history[pl.ds(8 * v + t, 24, stride=THICK), :] = roll(part, offset - HEIGHT * t, 1)


def split(values):
    high = values.astype(jnp.bfloat16)
    rest = values - high.astype(jnp.float32)
    mid = rest.astype(jnp.bfloat16)
    low = (rest - mid.astype(jnp.float32)).astype(jnp.bfloat16)
    return high, mid, low


def pick(values, one_hot, transposed):
    dims = (((1,), (1 if transposed else 0,)), ((), ()))
    total = None
    for part in split(values):
        term = lax.dot_general(part, one_hot, dims, preferred_element_type=jnp.float32)
        total = term if total is None else total + term
    return total


def pairing(match):
    return jnp.where(iota((FLAT, FLAT), 0) == match[...], 1.0, 0.0).astype(jnp.bfloat16)


def sweep(data, sends, w):
    w["load"][...] = jnp.zeros_like(w["load"])

    def one(step, carry):
        record(step, data, sends, w)
        update(w)
        return carry

    lax.fori_loop(0, STEPS - 1, one, 0)
    record(STEPS - 1, data, sends, w)


STATE = ("cur", "vel", "along_a", "along_h", "along_k", "keep", "faces", "inject", "load",
         "g_west", "g_east", "send_west", "send_east")


def state_shapes():
    block = (8, ARC)
    shapes = (
        (HEIGHT, COMPS * LAYERS) + block,
        (HEIGHT, COMPS * LAYERS) + block,
        (HEIGHT, LAYERS) + block,
        (HEIGHT, LAYERS) + block,
        (HEIGHT, LAYERS) + block,
        (HEIGHT, LAYERS) + block,
        (4, LAYERS) + block,
        (4, COMPS * LAYERS) + block,
        (COMPS * LAYERS,) + block,
        (PAD_ROWS, ARC),
        (PAD_ROWS, ARC),
        (PAD_ROWS, ARC),
        (PAD_ROWS, ARC),
    )
    return [pltpu.VMEM(shape, jnp.float32) for shape in shapes]


def clear_tail(w):
    tail = jnp.zeros((PAD_ROWS - FACE_ROWS, ARC), jnp.float32)
    for name in ("send_west", "send_east"):
        w[name][FACE_ROWS:, :] = tail


def first_kernel(disp, velocity, modulus, circ, rising, match, to_left, to_right, to_south, to_north, *scratch):
    w = dict(zip(STATE, scratch))
    prepare(disp, velocity, modulus, w)
    clear_tail(w)
    w["g_west"][0:FACE_ROWS, 0:HEIGHT] = circ[0:FACE_ROWS, :]
    w["g_east"][0:FACE_ROWS, 0:HEIGHT] = circ[FACE_ROWS : 2 * FACE_ROWS, :]
    w["g_east"][0:FACE_ROWS, :] = roll(w["g_east"][0:FACE_ROWS, :], -1, 1)
    sweep((rising, 0, rising, FACE_ROWS), (to_south, to_north), w)
    to_left[...] = pick(gather_rows(w["send_west"], 0), pairing(match), True)
    to_right[...] = gather_rows(w["send_east"], -1)


def second_kernel(
    disp, velocity, modulus, from_left, from_right, south, north, match, owner,
    disp_end, to_left, to_right, to_south, to_north, shares, *scratch
):
    w = dict(zip(STATE, scratch))
    prepare(disp, velocity, modulus, w)
    clear_tail(w)
    one_hot = pairing(match)
    scatter_rows(pick(from_left[...], one_hot, False), w["g_west"], 0)
    scatter_rows(from_right[...], w["g_east"], -1)
    sweep((south, 0, north, 0), (to_south, to_north), w)
    for c in range(COMPS):
        for l in range(LAYERS):
            w["send_east"][thickness_rows(FACE_ROWS + c * THICK, l), :] = w["load"][c * LAYERS + l]
    to_left[...] = pick(gather_rows(w["send_west"], 0), one_hot, True)
    east = gather_rows(w["send_east"], -1)
    to_right[...] = east
    owners = owner[...]
    device = owners // PATCH_DEV
    spot = owners - device * PATCH_DEV
    holder = jnp.where(iota((DEVICES, FLAT), 0) == device, 1.0, 0.0).astype(jnp.bfloat16)
    at = iota((PATCH_DEV, FLAT), 0) == spot
    terms = [
        jnp.where(at, east[LOAD_ROW + c : LOAD_ROW + c + 1, :], 0.0) for c in range(COMPS)
    ]
    terms.append(jnp.zeros((PATCH_DEV, FLAT), jnp.float32))
    total = None
    for part in split(jnp.concatenate(terms, axis=0)):
        term = lax.dot_general(holder, part, (((1,), (1,)), ((), ())), preferred_element_type=jnp.float32)
        total = term if total is None else total + term
    shares[...] = total
    update(w)
    for h in range(HEIGHT):
        for c in range(COMPS):
            for l in range(LAYERS):
                rows = thickness_rows(c * THICK * HEIGHT + h, l, HEIGHT)
                disp_end[rows, :] = roll(w["cur"][h, c * LAYERS + l], -h, 1)


def third_kernel(from_left, from_right, south, north, match, shares, circ_next, height_next, patch_load, rows, sems):
    copies = [
        pltpu.make_async_copy(south, height_next.at[pl.ds(0, FACE_ROWS)], sems.at[0]),
        pltpu.make_async_copy(north, height_next.at[pl.ds(FACE_ROWS, FACE_ROWS)], sems.at[1]),
    ]
    for copy in copies:
        copy.start()
    scatter_rows(pick(from_left[...], pairing(match), False), rows, 0)
    circ_next[0:FACE_ROWS, :] = rows[0:FACE_ROWS, 0:HEIGHT]
    scatter_rows(from_right[...], rows, 0)
    circ_next[FACE_ROWS : 2 * FACE_ROWS, :] = rows[0:FACE_ROWS, 0:HEIGHT]
    total = jnp.sum(shares[...], axis=0, keepdims=True)
    for c in range(COMPS):
        patch_load[c : c + 1, :] = total[:, c * PATCH_DEV : (c + 1) * PATCH_DEV]
    for copy in copies:
        copy.wait()


def f32(*shape):
    return jax.ShapeDtypeStruct(shape, jnp.float32)


PARAMS = pltpu.CompilerParams(vmem_limit_bytes=24 * 1024 * 1024)
VMEM = pl.BlockSpec(memory_space=pltpu.VMEM)
ANY = pl.BlockSpec(memory_space=pl.ANY)


def routed(to_left, to_right, to_south, to_north):
    blks, spans = lax.axis_size("blk"), lax.axis_size("span")
    south = lax.ppermute(to_north, "span", [(i, i + 1) for i in range(spans - 1)])
    north = lax.ppermute(to_south, "span", [(i + 1, i) for i in range(spans - 1)])
    west = lax.ppermute(to_right, "blk", [(i, (i + 1) % blks) for i in range(blks)])
    east = lax.ppermute(to_left, "blk", [((i + 1) % blks, i) for i in range(blks)])
    return west, east, south, north


def local(disp, velocity, modulus, guess_circ, guess_height, pair_match, patch_owner):
    disp = disp.reshape(COMPS * FLAT, ARC)
    velocity = velocity.reshape(COMPS * FLAT, ARC)
    modulus = modulus.reshape(FLAT, ARC)
    circ = guess_circ.reshape(2 * FACE_ROWS, HEIGHT)
    rising = guess_height.reshape(2 * FACE_ROWS, ARC)
    match = pair_match.reshape(1, FLAT)
    owner = patch_owner.reshape(1, FLAT)
    face = f32(FACE_ROWS, ARC)
    flat = f32(24, FLAT)
    sends = pl.pallas_call(
        first_kernel,
        out_shape=(flat, flat, face, face),
        in_specs=[VMEM] * 6,
        out_specs=(VMEM,) * 4,
        scratch_shapes=state_shapes(),
        compiler_params=PARAMS,
    )(disp, velocity, modulus, circ, rising, match)
    west, east, south, north = routed(*sends)
    disp_end, *sends, shares = pl.pallas_call(
        second_kernel,
        out_shape=(f32(COMPS * FLAT, ARC), flat, flat, face, face, f32(DEVICES, ARC)),
        in_specs=[VMEM] * 9,
        out_specs=(VMEM,) * 6,
        scratch_shapes=state_shapes(),
        compiler_params=PARAMS,
    )(disp, velocity, modulus, west, east, south, north, match, owner)
    west, east, south, north = routed(*sends)
    shares = lax.all_to_all(shares, ("blk", "span"), split_axis=0, concat_axis=0, tiled=True)
    circ_next, height_next, patch_load = pl.pallas_call(
        third_kernel,
        out_shape=(f32(2 * FACE_ROWS, HEIGHT), f32(2 * FACE_ROWS, ARC), f32(COMPS, PATCH_DEV)),
        in_specs=[VMEM, VMEM, ANY, ANY, VMEM, VMEM],
        out_specs=(VMEM, ANY, VMEM),
        scratch_shapes=[pltpu.VMEM((PAD_ROWS, ARC), jnp.float32), pltpu.SemaphoreType.DMA((2,))],
        compiler_params=PARAMS,
    )(west, east, south, north, match, shares)
    return (
        disp_end.reshape(COMPS, THICK, HEIGHT, ARC),
        circ_next.reshape(1, 2, STEPS, COMPS, THICK, HEIGHT),
        height_next.reshape(1, 2, STEPS, COMPS, THICK, ARC),
        patch_load,
    )


def solution(mesh):
    in_specs = (
        P(None, None, "span", "blk"),
        P(None, None, "span", "blk"),
        P(None, "span", "blk"),
        P("blk", None, None, None, None, "span"),
        P("span", None, None, None, None, "blk"),
        P("blk", "span", None),
        P("blk", "span", None),
    )
    out_specs = (
        P(None, None, "span", "blk"),
        P("blk", None, None, None, None, "span"),
        P("span", None, None, None, None, "blk"),
        P(None, ("blk", "span")),
    )
    return jax.shard_map(local, mesh=mesh, in_specs=in_specs, out_specs=out_specs, check_vma=False)
```

```python
import jax
import jax.numpy as jnp
from jax import lax
from jax.experimental import pallas as pl
from jax.experimental.pallas import tpu as pltpu
from jax.sharding import PartitionSpec as P

STEPS = 6
COMPS = 3
THICK = 24
HEIGHT = 16
ARC = 128
FLAT = THICK * HEIGHT
LAYERS = 3
FACE_ROWS = STEPS * COMPS * THICK
PAD_ROWS = 8 * COMPS * THICK
LOAD_ROW = STEPS * COMPS
PATCH_DEV = 32
DEVICES = 128


def roll(values, shift, axis):
    shift %= values.shape[axis]
    return values if shift == 0 else pltpu.roll(values, shift, axis)


def iota(shape, axis):
    return lax.broadcasted_iota(jnp.int32, shape, axis)


def thickness_rows(first, layer, stride=1):
    return pl.ds(first + layer * stride, 8, stride=LAYERS * stride)


def coefficients(modulus, w):
    lane = iota((8, ARC), 1)
    sub = iota((8, ARC), 0)
    zero = jnp.zeros((8, ARC), jnp.float32)
    moduli = [
        roll(modulus[thickness_rows(0, l, HEIGHT), :], 0, 1) for l in range(LAYERS)
    ]
    west = [zero] * LAYERS
    east = [zero] * LAYERS
    for h in range(HEIGHT):
        on_west = lane == h
        on_east = lane == (h - 1) % ARC
        if h + 1 < HEIGHT:
            above = [
                roll(modulus[thickness_rows(h + 1, l, HEIGHT), :], h + 1, 1) for l in range(LAYERS)
            ]
        for l in range(LAYERS):
            m = moduli[l]
            w["along_a"][h, l] = jnp.where(on_east, 0.0, 0.02 * (m + roll(m, -1, 1)))
            if l + 1 < LAYERS:
                w["along_k"][h, l] = 0.02 * (m + moduli[l + 1])
            else:
                w["along_k"][h, l] = jnp.where(sub == 7, 0.0, 0.02 * (m + roll(moduli[0], -1, 0)))
            if h + 1 < HEIGHT:
                w["along_h"][h, l] = 0.02 * (m + roll(above[l], -1, 1))
            imp = jnp.sqrt(m)
            damp = jnp.where(on_west | on_east, imp, 0.0)
            if h == 0:
                damp = damp + imp
                w["faces"][2, l] = 5.0 * imp
            if h == HEIGHT - 1:
                damp = damp + imp
                w["faces"][3, l] = 5.0 * imp
            w["keep"][h, l] = 1.0 - 0.2 * damp
            west[l] = jnp.where(on_west, 5.0 * imp, west[l])
            east[l] = jnp.where(on_east, 5.0 * imp, east[l])
        if h + 1 < HEIGHT:
            moduli = above
    for l in range(LAYERS):
        w["faces"][0, l] = west[l]
        w["faces"][1, l] = east[l]


def load_state(source, scale, kept, used):
    for h in range(HEIGHT):
        for c in range(COMPS):
            for l in range(LAYERS):
                rows = thickness_rows(c * THICK * HEIGHT + h, l, HEIGHT)
                values = source[rows, :]
                if scale != 1.0:
                    values = scale * values
                values = roll(values, h, 1)
                kept[h, c * LAYERS + l] = values
                used[h, c * LAYERS + l] = values


def sides():
    east = lax.axis_index("blk") % 2 == 0
    span = lax.axis_index("span")
    north = span % 2 == 0
    inner = (span > 0) & (span + 1 < lax.axis_size("span"))
    return east, north, inner


def record(step, data, sends, w):
    south_of, north_of = data
    send_first, send_second = sends
    _, to_north, inner = sides()
    weight = jnp.where(inner, 1.0, 0.0)
    lane = iota((8, ARC), 1)
    zero = jnp.zeros((8, ARC), jnp.float32)
    for c in range(COMPS):
        for l in range(LAYERS):
            b = c * LAYERS + l
            west, east = zero, zero
            for h in range(HEIGHT):
                v = w["vel"][h, b]
                west = jnp.where(lane == h, v, west)
                east = jnp.where(lane == (h - 1) % ARC, v, east)
            rows = thickness_rows(step * (COMPS * THICK) + c * THICK, l)
            g = w["g_west"][rows, :]
            w["inject"][0, b] = 0.04 * g
            w["send_west"][rows, :] = 2.0 * (w["faces"][0, l] * west) - g
            g = w["g_east"][rows, :]
            w["inject"][1, b] = 0.04 * g
            rate = w["faces"][1, l] * east
            w["send_east"][rows, :] = 2.0 * rate - g
            w["load"][b] = w["load"][b] + (g - rate)
            g = south_of(rows, step * (COMPS * THICK) + c * THICK, l)
            w["inject"][2, b] = 0.04 * g
            south = 2.0 * (w["faces"][2, l] * w["vel"][0, b]) - g
            g = north_of(rows, step * (COMPS * THICK) + c * THICK, l)
            w["inject"][3, b] = roll(0.04 * g, HEIGHT - 1, 1)
            rate = w["faces"][3, l] * w["vel"][HEIGHT - 1, b]
            north = roll(2.0 * rate, 1 - HEIGHT, 1) - g
            send_first[rows, :] = jnp.where(to_north, north, south)
            send_second[rows, :] = weight * jnp.where(to_north, south, north)


def update(w, from_cur=None, from_vel=None, sink=None):
    from_cur = w["cur"] if from_cur is None else from_cur
    from_vel = w["vel"] if from_vel is None else from_vel
    lane = iota((8, ARC), 1)
    blocks = [(c, l) for c in range(COMPS) for l in range(LAYERS)]
    cur = {b: from_cur[0, b[0] * LAYERS + b[1]] for b in blocks}
    left = {b: roll(cur[b], -1, 1) for b in blocks}
    rising = {}
    for h in range(HEIGHT):
        on_west = lane == h
        on_edge = on_west | (lane == (h - 1) % ARC)
        last = h + 1 == HEIGHT
        cur_next, left_next = {}, {}
        for c in range(COMPS):
            flux_k = []
            for l in range(LAYERS):
                here = cur[c, l]
                over = cur[c, l + 1] if l + 1 < LAYERS else roll(cur[c, 0], -1, 0)
                flux_k.append(w["along_k"][h, l] * (over - here))
            for l in range(LAYERS):
                b = (c, l)
                at = c * LAYERS + l
                here = cur[b]
                flux_a = w["along_a"][h, l] * (left[b] - here)
                total = flux_k[l] - (flux_k[l - 1] if l else roll(flux_k[LAYERS - 1], 1, 0))
                back = flux_a
                if h:
                    back = back + rising[b]
                total = total + flux_a - roll(back, 1, 1)
                if not last:
                    cur_next[b] = from_cur[h + 1, at]
                    left_next[b] = roll(cur_next[b], -1, 1)
                    rising[b] = w["along_h"][h, l] * (left_next[b] - here)
                    total = total + rising[b]
                g = jnp.where(on_west, w["inject"][0, at], w["inject"][1, at])
                total = total + jnp.where(on_edge, g, 0.0)
                if h == 0:
                    total = total + w["inject"][2, at]
                if last:
                    total = total + w["inject"][3, at]
                v = w["keep"][h, l] * from_vel[h, at] + total
                if sink is None:
                    w["vel"][h, at] = v
                    w["cur"][h, at] = here + v
                else:
                    sink(h, at, here + v)
        cur, left = cur_next, left_next


def gather_rows(history, offset):
    lane = iota((24, ARC), 1)
    parts = []
    for v in range(3):
        part = None
        for t in range(8):
            rows = roll(history[pl.ds(8 * v + t, 24, stride=THICK), :], HEIGHT * t - offset, 1)
            part = rows if part is None else jnp.where(lane >= HEIGHT * t, rows, part)
        parts.append(part)
    return jnp.concatenate(parts, axis=1)


def scatter_rows(flat, history, offset):
    for v in range(3):
        part = flat[:, v * ARC : (v + 1) * ARC]
        for t in range(8):
            history[pl.ds(8 * v + t, 24, stride=THICK), :] = roll(part, offset - HEIGHT * t, 1)


def split(values):
    high = values.astype(jnp.bfloat16)
    rest = values - high.astype(jnp.float32)
    mid = rest.astype(jnp.bfloat16)
    low = (rest - mid.astype(jnp.float32)).astype(jnp.bfloat16)
    return high, mid, low


def pick(values, one_hot, transposed):
    dims = (((1,), (1 if transposed else 0,)), ((), ()))
    total = None
    for part in split(values):
        term = lax.dot_general(part, one_hot, dims, preferred_element_type=jnp.float32)
        total = term if total is None else total + term
    return total


def pairing(match):
    return jnp.where(iota((FLAT, FLAT), 0) == match[...], 1.0, 0.0).astype(jnp.bfloat16)


def sweep(data, sends, w):
    w["load"][...] = jnp.zeros_like(w["load"])

    def one(step, carry):
        record(step, data, sends, w)
        update(w)
        return carry

    lax.fori_loop(0, STEPS - 1, one, 0)
    record(STEPS - 1, data, sends, w)


WORK = ("inject", "load", "g_west", "g_east", "send_west", "send_east")
COEFFICIENTS = ("along_a", "along_h", "along_k", "keep", "faces")
BLOCK = (8, ARC)
STATE_SHAPE = (HEIGHT, COMPS * LAYERS) + BLOCK
COEFFICIENT_SHAPES = ((HEIGHT, LAYERS) + BLOCK,) * 4 + ((4, LAYERS) + BLOCK,)
INJECT_SHAPE = (4, COMPS * LAYERS) + BLOCK


def work_shapes():
    shapes = (INJECT_SHAPE, (COMPS * LAYERS,) + BLOCK) + ((PAD_ROWS, ARC),) * 4
    return [pltpu.VMEM(shape, jnp.float32) for shape in shapes]


def clear_tail(w):
    tail = jnp.zeros((PAD_ROWS - FACE_ROWS, ARC), jnp.float32)
    for name in ("send_west", "send_east"):
        w[name][FACE_ROWS:, :] = tail


def spread_guess(circ, side, history, offset):
    rows = STEPS * COMPS * HEIGHT
    unit = jnp.where(iota((THICK, THICK), 0) == iota((THICK, THICK), 1), 1.0, 0.0).astype(jnp.bfloat16)
    total = None
    for part in split(circ[side * rows : (side + 1) * rows, :]):
        term = lax.dot_general(unit, part, (((1,), (1,)), ((), ())), preferred_element_type=jnp.float32)
        total = term if total is None else total + term
    total = jnp.concatenate([total, jnp.zeros((THICK, 3 * ARC - rows), jnp.float32)], axis=1)
    for i in range(STEPS * COMPS):
        tile = total[:, i // 8 * ARC : (i // 8 + 1) * ARC]
        history[i * THICK : (i + 1) * THICK, :] = roll(tile, offset - HEIGHT * (i % 8), 1)


def first_kernel(disp, velocity, modulus, circ, rising, pair_match, patch_owner, *refs):
    first_c, second_c, first_h, second_h, match, owner, cur0, vel0 = refs[:8]
    w = dict(zip(COEFFICIENTS, refs[8:13]))
    disp_in, velocity_in, modulus_in, circ_in, rising_in, sems, w["cur"], w["vel"] = refs[13:21]
    w.update(zip(WORK, refs[21:]))
    copies = [
        pltpu.make_async_copy(source, target, sems.at[i])
        for i, (source, target) in enumerate(
            (
                (modulus, modulus_in),
                (velocity, velocity_in),
                (disp, disp_in),
                (circ, circ_in),
                (rising, rising_in),
                (pair_match, match),
                (patch_owner, owner),
            )
        )
    ]
    for copy in copies:
        copy.start()
    clear_tail(w)
    copies[0].wait()
    coefficients(modulus_in, w)
    copies[1].wait()
    load_state(velocity_in, 0.2, vel0, w["vel"])
    copies[2].wait()
    load_state(disp_in, 1.0, cur0, w["cur"])
    copies[3].wait()
    spread_guess(circ_in, 0, w["g_west"], 0)
    spread_guess(circ_in, 1, w["g_east"], -1)
    for copy in copies[4:]:
        copy.wait()
    data = (
        lambda rows, at, l: rising_in[thickness_rows(at, l), :],
        lambda rows, at, l: rising_in[thickness_rows(FACE_ROWS + at, l), :],
    )
    sweep(data, (first_h, second_h), w)
    west = pick(gather_rows(w["send_west"], 0), pairing(match), True)
    east = gather_rows(w["send_east"], -1)
    to_east, _, _ = sides()
    first_c[...] = jnp.where(to_east, east, west)
    second_c[...] = jnp.where(to_east, west, east)


def second_kernel(got_first_c, got_second_c, got_first_h, got_second_h, match, owner, cur0, vel0, *refs):
    w = dict(zip(COEFFICIENTS, refs[:5]))
    first_c, second_c, first_h, second_h, shares, inject, w["cur"], w["vel"] = refs[5:13]
    w.update(zip(WORK, (inject,) + refs[13:]))
    clear_tail(w)
    one_hot = pairing(match)
    to_east, to_north, _ = sides()
    first, second = got_first_c[...], got_second_c[...]
    scatter_rows(pick(jnp.where(to_east, second, first), one_hot, False), w["g_west"], 0)
    scatter_rows(jnp.where(to_east, first, second), w["g_east"], -1)
    data = (
        lambda rows, at, l: jnp.where(to_north, got_second_h[rows, :], got_first_h[rows, :]),
        lambda rows, at, l: jnp.where(to_north, got_first_h[rows, :], got_second_h[rows, :]),
    )
    sweep(data, (first_h, second_h), w)
    for c in range(COMPS):
        for l in range(LAYERS):
            w["send_east"][thickness_rows(FACE_ROWS + c * THICK, l), :] = w["load"][c * LAYERS + l]
    west = pick(gather_rows(w["send_west"], 0), one_hot, True)
    east = gather_rows(w["send_east"], -1)
    first_c[...] = jnp.where(to_east, east, west)
    second_c[...] = jnp.where(to_east, west, east)
    owners = owner[...]
    device = owners // PATCH_DEV
    spot = owners - device * PATCH_DEV
    holder = jnp.where(iota((DEVICES, FLAT), 0) == device, 1.0, 0.0).astype(jnp.bfloat16)
    at = iota((PATCH_DEV, FLAT), 0) == spot
    terms = [
        jnp.where(at, east[LOAD_ROW + c : LOAD_ROW + c + 1, :], 0.0) for c in range(COMPS)
    ]
    terms.append(jnp.zeros((PATCH_DEV, FLAT), jnp.float32))
    total = None
    for part in split(jnp.concatenate(terms, axis=0)):
        term = lax.dot_general(holder, part, (((1,), (1,)), ((), ())), preferred_element_type=jnp.float32)
        total = term if total is None else total + term
    shares[...] = total


def last_kernel(got_first_c, got_second_c, got_first_h, got_second_h, match, cur, vel, inject, *refs):
    w = dict(zip(COEFFICIENTS, refs[:5]))
    disp_end, circ_next, height_next, ending, end_rows, turned_rows, circ_rows, sems = refs[5:]
    w["inject"] = inject
    to_east, to_north, _ = sides()
    first_at = pl.multiple_of(jnp.where(to_north, FACE_ROWS, 0), 8)
    second_at = pl.multiple_of(jnp.where(to_north, 0, FACE_ROWS), 8)
    copies = [
        pltpu.make_async_copy(got_first_h, height_next.at[pl.ds(first_at, FACE_ROWS)], sems.at[0]),
        pltpu.make_async_copy(got_second_h, height_next.at[pl.ds(second_at, FACE_ROWS)], sems.at[1]),
        pltpu.make_async_copy(end_rows, disp_end, sems.at[2]),
        pltpu.make_async_copy(circ_rows, circ_next, sems.at[3]),
    ]
    copies[0].start()
    copies[1].start()

    def keep_end(h, at, values):
        ending[h, at] = values

    update(w, cur, vel, keep_end)
    for h in range(HEIGHT):
        for c in range(COMPS):
            for l in range(LAYERS):
                rows = thickness_rows(c * THICK * HEIGHT + h, l, HEIGHT)
                end_rows[rows, :] = roll(ending[h, c * LAYERS + l], -h, 1)
    copies[2].start()
    first, second = got_first_c[...], got_second_c[...]
    west = pick(jnp.where(to_east, second, first), pairing(match), False)
    east = jnp.where(to_east, first, second)
    lanes = 32 * HEIGHT
    spot = iota((FLAT, lanes), 1)
    k, h = spot % 32, spot // 32
    turn = jnp.where((iota((FLAT, lanes), 0) == k * HEIGHT + h) & (k < THICK), 1.0, 0.0).astype(jnp.bfloat16)
    turned = pick(jnp.concatenate([west, east], axis=0), turn, False)
    face = STEPS * COMPS * HEIGHT
    for side in range(2):
        part = turned[24 * side : 24 * (side + 1), :]
        for h in range(HEIGHT):
            tile = part[:, h // 4 * ARC : (h // 4 + 1) * ARC]
            turned_rows[pl.ds(24 * HEIGHT * side + h, 24, stride=HEIGHT), :] = roll(tile, -32 * (h % 4), 1)
        first_row = 24 * HEIGHT * side
        circ_rows[face * side : face * (side + 1), :] = turned_rows[first_row : first_row + face, 0:THICK]
    copies[3].start()
    for copy in copies:
        copy.wait()


def sum_kernel(shares, _, patch_load):
    total = jnp.sum(shares[...], axis=0, keepdims=True)
    for c in range(COMPS):
        patch_load[c : c + 1, :] = total[:, c * PATCH_DEV : (c + 1) * PATCH_DEV]


def f32(*shape):
    return jax.ShapeDtypeStruct(shape, jnp.float32)


PARAMS = pltpu.CompilerParams(vmem_limit_bytes=24 * 1024 * 1024)
VMEM = pl.BlockSpec(memory_space=pltpu.VMEM)
ANY = pl.BlockSpec(memory_space=pl.ANY)
HBM = pl.BlockSpec(memory_space=pltpu.HBM)


def exchanged(first_c, second_c, first_h, second_h):
    blks, spans = lax.axis_size("blk"), lax.axis_size("span")

    def pairs(count, start):
        return [p for i in range(start, count, 2) for p in ((i, (i + 1) % count), ((i + 1) % count, i))]

    first_h = lax.ppermute(first_h, "span", pairs(spans, 0))
    second_h = lax.ppermute(second_h, "span", pairs(spans, 1))
    first_c = lax.ppermute(first_c, "blk", pairs(blks, 0))
    second_c = lax.ppermute(second_c, "blk", pairs(blks, 1))
    return first_c, second_c, first_h, second_h


def local(disp, velocity, modulus, guess_circ, guess_height, pair_match, patch_owner):
    disp = disp.reshape(COMPS * FLAT, ARC)
    velocity = velocity.reshape(COMPS * FLAT, ARC)
    modulus = modulus.reshape(FLAT, ARC)
    side_rows = STEPS * COMPS * HEIGHT
    circ = jnp.swapaxes(guess_circ, 4, 5).reshape(2 * side_rows, THICK)
    rising = guess_height.reshape(2 * FACE_ROWS, ARC)
    match = pair_match.reshape(1, FLAT)
    owner = patch_owner.reshape(1, FLAT)
    face = f32(FACE_ROWS, ARC)
    flat = f32(24, FLAT)
    state = f32(*STATE_SHAPE)
    copied = ((COMPS * FLAT, ARC), (COMPS * FLAT, ARC), (FLAT, ARC), (2 * side_rows, THICK), (2 * FACE_ROWS, ARC))
    row = jax.ShapeDtypeStruct((1, FLAT), jnp.int32)
    inputs = (disp, velocity, modulus, circ, rising, match, owner)
    *sends, match, owner, cur, vel, k1, k2, k3, k4, k5 = pl.pallas_call(
        first_kernel,
        out_shape=(flat, flat, face, face, row, row, state, state) + tuple(f32(*shape) for shape in COEFFICIENT_SHAPES),
        in_specs=[HBM] * 7,
        out_specs=(VMEM,) * 13,
        scratch_shapes=[pltpu.VMEM(shape, jnp.float32) for shape in copied]
        + [pltpu.SemaphoreType.DMA((7,))]
        + [pltpu.VMEM(STATE_SHAPE, jnp.float32)] * 2
        + work_shapes(),
        compiler_params=PARAMS,
    )(*(pltpu.with_memory_space_constraint(x, pltpu.HBM) for x in inputs))
    coefficient = (k1, k2, k3, k4, k5)
    got = exchanged(*sends)
    *sends, shares, inject, cur, vel = pl.pallas_call(
        second_kernel,
        out_shape=(flat, flat, face, face, f32(DEVICES, ARC), f32(*INJECT_SHAPE), state, state),
        in_specs=[VMEM] * 13,
        out_specs=(VMEM,) * 8,
        scratch_shapes=work_shapes()[1:],
        input_output_aliases={6: 6, 7: 7},
        compiler_params=PARAMS,
    )(*got, match, owner, cur, vel, *coefficient)
    got = exchanged(*sends)
    shares = lax.all_to_all(shares, ("blk", "span"), split_axis=0, concat_axis=0, tiled=True)
    disp_end, circ_next, height_next = pl.pallas_call(
        last_kernel,
        out_shape=(f32(COMPS * FLAT, ARC), f32(2 * side_rows, THICK), f32(2 * FACE_ROWS, ARC)),
        in_specs=[VMEM, VMEM, ANY, ANY] + [VMEM] * 9,
        out_specs=(ANY,) * 3,
        scratch_shapes=[
            pltpu.VMEM(STATE_SHAPE, jnp.float32),
            pltpu.VMEM((COMPS * FLAT, ARC), jnp.float32),
            pltpu.VMEM((2 * 24 * HEIGHT, ARC), jnp.float32),
            pltpu.VMEM((2 * side_rows, THICK), jnp.float32),
            pltpu.SemaphoreType.DMA((4,)),
        ],
        compiler_params=PARAMS,
    )(*got, match, cur, vel, inject, *coefficient)
    patch_load = pl.pallas_call(
        sum_kernel, out_shape=f32(COMPS, PATCH_DEV), in_specs=[VMEM, ANY], out_specs=VMEM, compiler_params=PARAMS
    )(shares, pltpu.with_memory_space_constraint(circ_next, pltpu.HBM))
    circ_next = circ_next.reshape(1, 2, STEPS, COMPS, HEIGHT, THICK)
    return (
        disp_end.reshape(COMPS, THICK, HEIGHT, ARC),
        jnp.swapaxes(circ_next, 4, 5),
        height_next.reshape(1, 2, STEPS, COMPS, THICK, ARC),
        patch_load,
    )


def solution(mesh):
    in_specs = (
        P(None, None, "span", "blk"),
        P(None, None, "span", "blk"),
        P(None, "span", "blk"),
        P("blk", None, None, None, None, "span"),
        P("span", None, None, None, None, "blk"),
        P("blk", "span", None),
        P("blk", "span", None),
    )
    out_specs = (
        P(None, None, "span", "blk"),
        P("blk", None, None, None, None, "span"),
        P("span", None, None, None, None, "blk"),
        P(None, ("blk", "span")),
    )
    return jax.shard_map(local, mesh=mesh, in_specs=in_specs, out_specs=out_specs, check_vma=False)
```

```python
import jax
import jax.numpy as jnp
from jax import lax
from jax.experimental import pallas as pl
from jax.experimental.pallas import tpu as pltpu
from jax.sharding import PartitionSpec as P

STEPS = 6
COMPS = 3
THICK = 24
HEIGHT = 16
ARC = 128
FLAT = THICK * HEIGHT
LAYERS = 3
FACE_ROWS = STEPS * COMPS * THICK
PAD_ROWS = 8 * COMPS * THICK
LOAD_ROW = STEPS * COMPS
PATCH_DEV = 32
DEVICES = 128


def roll(values, shift, axis):
    shift %= values.shape[axis]
    return values if shift == 0 else pltpu.roll(values, shift, axis)


def iota(shape, axis):
    return lax.broadcasted_iota(jnp.int32, shape, axis)


def thickness_rows(first, layer, stride=1):
    return pl.ds(first + layer * stride, 8, stride=LAYERS * stride)


def coefficients(modulus, w):
    lane = iota((8, ARC), 1)
    sub = iota((8, ARC), 0)
    zero = jnp.zeros((8, ARC), jnp.float32)
    moduli = [
        roll(modulus[thickness_rows(0, l, HEIGHT), :], 0, 1) for l in range(LAYERS)
    ]
    west = [zero] * LAYERS
    east = [zero] * LAYERS
    for h in range(HEIGHT):
        on_west = lane == h
        on_east = lane == (h - 1) % ARC
        if h + 1 < HEIGHT:
            above = [
                roll(modulus[thickness_rows(h + 1, l, HEIGHT), :], h + 1, 1) for l in range(LAYERS)
            ]
        for l in range(LAYERS):
            m = moduli[l]
            w["along_a"][h, l] = jnp.where(on_east, 0.0, 0.02 * (m + roll(m, -1, 1)))
            if l + 1 < LAYERS:
                w["along_k"][h, l] = 0.02 * (m + moduli[l + 1])
            else:
                w["along_k"][h, l] = jnp.where(sub == 7, 0.0, 0.02 * (m + roll(moduli[0], -1, 0)))
            if h + 1 < HEIGHT:
                w["along_h"][h, l] = 0.02 * (m + roll(above[l], -1, 1))
            imp = jnp.sqrt(m)
            damp = jnp.where(on_west | on_east, imp, 0.0)
            if h == 0:
                damp = damp + imp
                w["faces"][2, l] = 5.0 * imp
            if h == HEIGHT - 1:
                damp = damp + imp
                w["faces"][3, l] = 5.0 * imp
            w["keep"][h, l] = 1.0 - 0.2 * damp
            west[l] = jnp.where(on_west, 5.0 * imp, west[l])
            east[l] = jnp.where(on_east, 5.0 * imp, east[l])
        if h + 1 < HEIGHT:
            moduli = above
    for l in range(LAYERS):
        w["faces"][0, l] = west[l]
        w["faces"][1, l] = east[l]


def load_state(source, scale, kept, used):
    for h in range(HEIGHT):
        for c in range(COMPS):
            for l in range(LAYERS):
                rows = thickness_rows(c * THICK * HEIGHT + h, l, HEIGHT)
                values = source[rows, :]
                if scale != 1.0:
                    values = scale * values
                values = roll(values, h, 1)
                kept[h, c * LAYERS + l] = values
                used[h, c * LAYERS + l] = values


def sides():
    east = lax.axis_index("blk") % 2 == 0
    span = lax.axis_index("span")
    north = span % 2 == 0
    inner = (span > 0) & (span + 1 < lax.axis_size("span"))
    return east, north, inner


def face_rates(w):
    lane = iota((8, ARC), 1)
    zero = jnp.zeros((8, ARC), jnp.float32)

    def rates(c, l):
        b = c * LAYERS + l
        west, east = zero, zero
        for h in range(HEIGHT):
            v = w["vel"][h, b]
            west = jnp.where(lane == h, v, west)
            east = jnp.where(lane == (h - 1) % ARC, v, east)
        north = roll(w["faces"][3, l] * w["vel"][HEIGHT - 1, b], 1 - HEIGHT, 1)
        return w["faces"][0, l] * west, w["faces"][1, l] * east, w["faces"][2, l] * w["vel"][0, b], north

    return rates


def record(step, rates, data, sends, w):
    south_of, north_of = data
    send_first, send_second = sends
    _, to_north, inner = sides()
    weight = jnp.where(inner, 1.0, 0.0)
    for c in range(COMPS):
        for l in range(LAYERS):
            b = c * LAYERS + l
            rate_west, rate_east, rate_south, rate_north = rates(c, l)
            rows = thickness_rows(step * (COMPS * THICK) + c * THICK, l)
            g = w["g_west"][rows, :]
            w["inject"][0, b] = 0.04 * g
            w["send_west"][rows, :] = 2.0 * rate_west - g
            g = w["g_east"][rows, :]
            w["inject"][1, b] = 0.04 * g
            w["send_east"][rows, :] = 2.0 * rate_east - g
            w["load"][b] = w["load"][b] + (g - rate_east)
            g = south_of(rows, step * (COMPS * THICK) + c * THICK, l)
            w["inject"][2, b] = 0.04 * g
            south = 2.0 * rate_south - g
            g = north_of(rows, step * (COMPS * THICK) + c * THICK, l)
            w["inject"][3, b] = roll(0.04 * g, HEIGHT - 1, 1)
            north = 2.0 * rate_north - g
            send_first[rows, :] = jnp.where(to_north, north, south)
            send_second[rows, :] = weight * jnp.where(to_north, south, north)


def injected(h, at, w):
    lane = iota((8, ARC), 1)
    on_west = lane == h
    on_edge = on_west | (lane == (h - 1) % ARC)
    g = jnp.where(on_edge, jnp.where(on_west, w["inject"][0, at], w["inject"][1, at]), 0.0)
    if h == 0:
        g = g + w["inject"][2, at]
    if h == HEIGHT - 1:
        g = g + w["inject"][3, at]
    return g


def update(w, from_cur=None, from_vel=None, sink=None, inject=True):
    from_cur = w["cur"] if from_cur is None else from_cur
    from_vel = w["vel"] if from_vel is None else from_vel
    blocks = [(c, l) for c in range(COMPS) for l in range(LAYERS)]
    cur = {b: from_cur[0, b[0] * LAYERS + b[1]] for b in blocks}
    left = {b: roll(cur[b], -1, 1) for b in blocks}
    rising = {}
    for h in range(HEIGHT):
        last = h + 1 == HEIGHT
        cur_next, left_next = {}, {}
        for c in range(COMPS):
            flux_k = []
            for l in range(LAYERS):
                here = cur[c, l]
                over = cur[c, l + 1] if l + 1 < LAYERS else roll(cur[c, 0], -1, 0)
                flux_k.append(w["along_k"][h, l] * (over - here))
            for l in range(LAYERS):
                b = (c, l)
                at = c * LAYERS + l
                here = cur[b]
                flux_a = w["along_a"][h, l] * (left[b] - here)
                total = flux_k[l] - (flux_k[l - 1] if l else roll(flux_k[LAYERS - 1], 1, 0))
                back = flux_a
                if h:
                    back = back + rising[b]
                total = total + flux_a - roll(back, 1, 1)
                if not last:
                    cur_next[b] = from_cur[h + 1, at]
                    left_next[b] = roll(cur_next[b], -1, 1)
                    rising[b] = w["along_h"][h, l] * (left_next[b] - here)
                    total = total + rising[b]
                if inject:
                    total = total + injected(h, at, w)
                v = w["keep"][h, l] * from_vel[h, at] + total
                if sink is None:
                    w["vel"][h, at] = v
                    w["cur"][h, at] = here + v
                else:
                    sink(h, at, here + v)
        cur, left = cur_next, left_next


def gather_rows(history, offset):
    lane = iota((24, ARC), 1)
    parts = []
    for v in range(3):
        part = None
        for t in range(8):
            rows = roll(history[pl.ds(8 * v + t, 24, stride=THICK), :], HEIGHT * t - offset, 1)
            part = rows if part is None else jnp.where(lane >= HEIGHT * t, rows, part)
        parts.append(part)
    return jnp.concatenate(parts, axis=1)


def scatter_rows(flat, history, offset):
    for v in range(3):
        part = flat[:, v * ARC : (v + 1) * ARC]
        for t in range(8):
            history[pl.ds(8 * v + t, 24, stride=THICK), :] = roll(part, offset - HEIGHT * t, 1)


def split(values):
    high = values.astype(jnp.bfloat16)
    rest = values - high.astype(jnp.float32)
    mid = rest.astype(jnp.bfloat16)
    low = (rest - mid.astype(jnp.float32)).astype(jnp.bfloat16)
    return high, mid, low


def pick(values, one_hot, transposed):
    dims = (((1,), (1 if transposed else 0,)), ((), ()))
    total = None
    for part in split(values):
        term = lax.dot_general(part, one_hot, dims, preferred_element_type=jnp.float32)
        total = term if total is None else total + term
    return total


def pairing(match):
    return jnp.where(iota((FLAT, FLAT), 0) == match[...], 1.0, 0.0).astype(jnp.bfloat16)


def sweep(first_step, data, sends, w):
    def one(step, carry):
        record(step, face_rates(w), data, sends, w)
        update(w)
        return carry

    lax.fori_loop(first_step, STEPS - 1, one, 0)
    record(STEPS - 1, face_rates(w), data, sends, w)


WORK = ("inject", "load", "g_west", "g_east", "send_west", "send_east")
COEFFICIENTS = ("along_a", "along_h", "along_k", "keep", "faces")
BLOCK = (8, ARC)
STATE_SHAPE = (HEIGHT, COMPS * LAYERS) + BLOCK
COEFFICIENT_SHAPES = ((HEIGHT, LAYERS) + BLOCK,) * 4 + ((4, LAYERS) + BLOCK,)
INJECT_SHAPE = (4, COMPS * LAYERS) + BLOCK


def work_shapes():
    shapes = (INJECT_SHAPE, (COMPS * LAYERS,) + BLOCK) + ((PAD_ROWS, ARC),) * 4
    return [pltpu.VMEM(shape, jnp.float32) for shape in shapes]


def clear_tail(w):
    tail = jnp.zeros((PAD_ROWS - FACE_ROWS, ARC), jnp.float32)
    for name in ("send_west", "send_east"):
        w[name][FACE_ROWS:, :] = tail


def spread_guess(circ, side, history, offset):
    rows = STEPS * COMPS * HEIGHT
    unit = jnp.where(iota((THICK, THICK), 0) == iota((THICK, THICK), 1), 1.0, 0.0).astype(jnp.bfloat16)
    total = None
    for part in split(circ[side * rows : (side + 1) * rows, :]):
        term = lax.dot_general(unit, part, (((1,), (1,)), ((), ())), preferred_element_type=jnp.float32)
        total = term if total is None else total + term
    total = jnp.concatenate([total, jnp.zeros((THICK, 3 * ARC - rows), jnp.float32)], axis=1)
    for i in range(STEPS * COMPS):
        tile = total[:, i // 8 * ARC : (i // 8 + 1) * ARC]
        history[i * THICK : (i + 1) * THICK, :] = roll(tile, offset - HEIGHT * (i % 8), 1)


def first_kernel(disp, velocity, modulus, circ, rising, pair_match, patch_owner, *refs):
    first_c, second_c, first_h, second_h, match, owner, cur0, vel0 = refs[:8]
    w = dict(zip(COEFFICIENTS, refs[8:13]))
    disp_in, velocity_in, modulus_in, circ_in, rising_in, sems, w["cur"], w["vel"] = refs[13:21]
    w.update(zip(WORK, refs[21:]))
    copies = [
        pltpu.make_async_copy(source, target, sems.at[i])
        for i, (source, target) in enumerate(
            (
                (modulus, modulus_in),
                (velocity, velocity_in),
                (disp, disp_in),
                (circ, circ_in),
                (rising, rising_in),
                (pair_match, match),
                (patch_owner, owner),
            )
        )
    ]
    for copy in copies:
        copy.start()
    clear_tail(w)
    copies[0].wait()
    coefficients(modulus_in, w)
    copies[1].wait()
    load_state(velocity_in, 0.2, vel0, w["vel"])
    copies[2].wait()
    load_state(disp_in, 1.0, cur0, w["cur"])
    copies[3].wait()
    spread_guess(circ_in, 0, w["g_west"], 0)
    spread_guess(circ_in, 1, w["g_east"], -1)
    for copy in copies[4:]:
        copy.wait()
    data = (
        lambda rows, at, l: rising_in[thickness_rows(at, l), :],
        lambda rows, at, l: rising_in[thickness_rows(FACE_ROWS + at, l), :],
    )
    w["load"][...] = jnp.zeros_like(w["load"])
    sweep(0, data, (first_h, second_h), w)
    west = pick(gather_rows(w["send_west"], 0), pairing(match), True)
    east = gather_rows(w["send_east"], -1)
    to_east, _, _ = sides()
    first_c[...] = jnp.where(to_east, east, west)
    second_c[...] = jnp.where(to_east, west, east)


def middle_kernel(match, cur0, vel0, *refs):
    w = dict(zip(COEFFICIENTS, refs[:5]))
    rates, one_hot, w["cur"], w["vel"] = refs[5:]
    one_hot[...] = pairing(match)
    of = face_rates(w)
    for c in range(COMPS):
        for l in range(LAYERS):
            for side, values in enumerate(of(c, l)):
                rates[side, c * LAYERS + l] = values
    update(w, inject=False)


def second_kernel(got_first_c, got_second_c, got_first_h, got_second_h, pairs, rates, owner, cur1, vel1, *refs):
    w = dict(zip(COEFFICIENTS, refs[:5]))
    first_c, second_c, first_h, second_h, shares, inject, w["cur"], w["vel"] = refs[5:13]
    w.update(zip(WORK, (inject,) + refs[13:]))
    clear_tail(w)
    one_hot = pairs[...]
    to_east, to_north, _ = sides()
    first, second = got_first_c[...], got_second_c[...]
    scatter_rows(pick(jnp.where(to_east, second, first), one_hot, False), w["g_west"], 0)
    scatter_rows(jnp.where(to_east, first, second), w["g_east"], -1)
    data = (
        lambda rows, at, l: jnp.where(to_north, got_second_h[rows, :], got_first_h[rows, :]),
        lambda rows, at, l: jnp.where(to_north, got_first_h[rows, :], got_second_h[rows, :]),
    )
    w["load"][...] = jnp.zeros_like(w["load"])
    record(0, lambda c, l: [rates[side, c * LAYERS + l] for side in range(4)], data, (first_h, second_h), w)
    for h in range(HEIGHT):
        for at in range(COMPS * LAYERS):
            g = injected(h, at, w)
            w["vel"][h, at] = w["vel"][h, at] + g
            w["cur"][h, at] = w["cur"][h, at] + g
    sweep(1, data, (first_h, second_h), w)
    for c in range(COMPS):
        for l in range(LAYERS):
            w["send_east"][thickness_rows(FACE_ROWS + c * THICK, l), :] = w["load"][c * LAYERS + l]
    west = pick(gather_rows(w["send_west"], 0), one_hot, True)
    east = gather_rows(w["send_east"], -1)
    first_c[...] = jnp.where(to_east, east, west)
    second_c[...] = jnp.where(to_east, west, east)
    owners = owner[...]
    device = owners // PATCH_DEV
    spot = owners - device * PATCH_DEV
    holder = jnp.where(iota((DEVICES, FLAT), 0) == device, 1.0, 0.0).astype(jnp.bfloat16)
    at = iota((PATCH_DEV, FLAT), 0) == spot
    terms = [
        jnp.where(at, east[LOAD_ROW + c : LOAD_ROW + c + 1, :], 0.0) for c in range(COMPS)
    ]
    terms.append(jnp.zeros((PATCH_DEV, FLAT), jnp.float32))
    total = None
    for part in split(jnp.concatenate(terms, axis=0)):
        term = lax.dot_general(holder, part, (((1,), (1,)), ((), ())), preferred_element_type=jnp.float32)
        total = term if total is None else total + term
    shares[...] = total


def end_kernel(cur, vel, inject, *refs):
    w = dict(zip(COEFFICIENTS, refs[:5]))
    disp_end, ending = refs[5:]
    w["inject"] = inject

    def keep_end(h, at, values):
        ending[h, at] = values

    update(w, cur, vel, keep_end)
    for h in range(HEIGHT):
        for c in range(COMPS):
            for l in range(LAYERS):
                rows = thickness_rows(c * THICK * HEIGHT + h, l, HEIGHT)
                disp_end[rows, :] = roll(ending[h, c * LAYERS + l], -h, 1)


def face_kernel(got_first_c, got_second_c, got_first_h, got_second_h, match, _, *refs):
    circ_next, height_next, turned_rows, sems = refs
    to_east, to_north, _ = sides()
    first_at = pl.multiple_of(jnp.where(to_north, FACE_ROWS, 0), 8)
    second_at = pl.multiple_of(jnp.where(to_north, 0, FACE_ROWS), 8)
    copies = [
        pltpu.make_async_copy(got_first_h, height_next.at[pl.ds(first_at, FACE_ROWS)], sems.at[0]),
        pltpu.make_async_copy(got_second_h, height_next.at[pl.ds(second_at, FACE_ROWS)], sems.at[1]),
    ]
    for copy in copies:
        copy.start()
    first, second = got_first_c[...], got_second_c[...]
    west = pick(jnp.where(to_east, second, first), pairing(match), False)
    east = jnp.where(to_east, first, second)
    lanes = 32 * HEIGHT
    spot = iota((FLAT, lanes), 1)
    k, h = spot % 32, spot // 32
    turn = jnp.where((iota((FLAT, lanes), 0) == k * HEIGHT + h) & (k < THICK), 1.0, 0.0).astype(jnp.bfloat16)
    turned = pick(jnp.concatenate([west, east], axis=0), turn, False)
    face = STEPS * COMPS * HEIGHT
    for side in range(2):
        part = turned[24 * side : 24 * (side + 1), :]
        for h in range(HEIGHT):
            tile = part[:, h // 4 * ARC : (h // 4 + 1) * ARC]
            turned_rows[pl.ds(24 * HEIGHT * side + h, 24, stride=HEIGHT), :] = roll(tile, -32 * (h % 4), 1)
        first_row = 24 * HEIGHT * side
        circ_next[face * side : face * (side + 1), :] = turned_rows[first_row : first_row + face, 0:THICK]
    for copy in copies:
        copy.wait()


def sum_kernel(shares, _, patch_load):
    total = jnp.sum(shares[...], axis=0, keepdims=True)
    for c in range(COMPS):
        patch_load[c : c + 1, :] = total[:, c * PATCH_DEV : (c + 1) * PATCH_DEV]


def f32(*shape):
    return jax.ShapeDtypeStruct(shape, jnp.float32)


PARAMS = pltpu.CompilerParams(vmem_limit_bytes=24 * 1024 * 1024)
VMEM = pl.BlockSpec(memory_space=pltpu.VMEM)
ANY = pl.BlockSpec(memory_space=pl.ANY)
HBM = pl.BlockSpec(memory_space=pltpu.HBM)


def exchanged(first_c, second_c, first_h, second_h):
    blks, spans = lax.axis_size("blk"), lax.axis_size("span")

    def pairs(count, start):
        return [p for i in range(start, count, 2) for p in ((i, (i + 1) % count), ((i + 1) % count, i))]

    first_h = lax.ppermute(first_h, "span", pairs(spans, 0))
    second_h = lax.ppermute(second_h, "span", pairs(spans, 1))
    first_c = lax.ppermute(first_c, "blk", pairs(blks, 0))
    second_c = lax.ppermute(second_c, "blk", pairs(blks, 1))
    return first_c, second_c, first_h, second_h


def local(disp, velocity, modulus, guess_circ, guess_height, pair_match, patch_owner):
    disp = disp.reshape(COMPS * FLAT, ARC)
    velocity = velocity.reshape(COMPS * FLAT, ARC)
    modulus = modulus.reshape(FLAT, ARC)
    side_rows = STEPS * COMPS * HEIGHT
    circ = jnp.swapaxes(guess_circ, 4, 5).reshape(2 * side_rows, THICK)
    rising = guess_height.reshape(2 * FACE_ROWS, ARC)
    match = pair_match.reshape(1, FLAT)
    owner = patch_owner.reshape(1, FLAT)
    face = f32(FACE_ROWS, ARC)
    flat = f32(24, FLAT)
    state = f32(*STATE_SHAPE)
    copied = ((COMPS * FLAT, ARC), (COMPS * FLAT, ARC), (FLAT, ARC), (2 * side_rows, THICK), (2 * FACE_ROWS, ARC))
    row = jax.ShapeDtypeStruct((1, FLAT), jnp.int32)
    inputs = (disp, velocity, modulus, circ, rising, match, owner)
    *sends, match, owner, cur, vel, k1, k2, k3, k4, k5 = pl.pallas_call(
        first_kernel,
        out_shape=(flat, flat, face, face, row, row, state, state) + tuple(f32(*shape) for shape in COEFFICIENT_SHAPES),
        in_specs=[HBM] * 7,
        out_specs=(VMEM,) * 13,
        scratch_shapes=[pltpu.VMEM(shape, jnp.float32) for shape in copied]
        + [pltpu.SemaphoreType.DMA((7,))]
        + [pltpu.VMEM(STATE_SHAPE, jnp.float32)] * 2
        + work_shapes(),
        compiler_params=PARAMS,
    )(*(pltpu.with_memory_space_constraint(x, pltpu.HBM) for x in inputs))
    coefficient = (k1, k2, k3, k4, k5)
    got = exchanged(*sends)
    rates, pairs, cur, vel = pl.pallas_call(
        middle_kernel,
        out_shape=(f32(*INJECT_SHAPE), jax.ShapeDtypeStruct((FLAT, FLAT), jnp.bfloat16), state, state),
        in_specs=[VMEM] * 8,
        out_specs=(VMEM,) * 4,
        input_output_aliases={1: 2, 2: 3},
        compiler_params=PARAMS,
        cost_estimate=pl.CostEstimate(flops=3 * 10**6, bytes_accessed=4 * 10**6, transcendentals=0),
    )(match, cur, vel, *coefficient)
    *sends, shares, inject, cur, vel = pl.pallas_call(
        second_kernel,
        out_shape=(flat, flat, face, face, f32(DEVICES, ARC), f32(*INJECT_SHAPE), state, state),
        in_specs=[VMEM] * 14,
        out_specs=(VMEM,) * 8,
        scratch_shapes=work_shapes()[1:],
        input_output_aliases={7: 6, 8: 7},
        compiler_params=PARAMS,
    )(*got, pairs, rates, owner, cur, vel, *coefficient)
    got = exchanged(*sends)
    shares = lax.all_to_all(shares, ("blk", "span"), split_axis=0, concat_axis=0, tiled=True)
    disp_end = pl.pallas_call(
        end_kernel,
        out_shape=f32(COMPS * FLAT, ARC),
        in_specs=[VMEM] * 8,
        out_specs=VMEM,
        scratch_shapes=[pltpu.VMEM(STATE_SHAPE, jnp.float32)],
        compiler_params=PARAMS,
    )(cur, vel, inject, *coefficient)
    circ_next, height_next = pl.pallas_call(
        face_kernel,
        out_shape=(f32(2 * side_rows, THICK), f32(2 * FACE_ROWS, ARC)),
        in_specs=[VMEM, VMEM, ANY, ANY, VMEM, ANY],
        out_specs=(VMEM, ANY),
        scratch_shapes=[pltpu.VMEM((2 * 24 * HEIGHT, ARC), jnp.float32), pltpu.SemaphoreType.DMA((2,))],
        compiler_params=PARAMS,
    )(*got, match, pltpu.with_memory_space_constraint(disp_end, pltpu.HBM))
    patch_load = pl.pallas_call(
        sum_kernel, out_shape=f32(COMPS, PATCH_DEV), in_specs=[VMEM, ANY], out_specs=VMEM, compiler_params=PARAMS
    )(shares, pltpu.with_memory_space_constraint(circ_next, pltpu.HBM))
    circ_next = circ_next.reshape(1, 2, STEPS, COMPS, HEIGHT, THICK)
    return (
        disp_end.reshape(COMPS, THICK, HEIGHT, ARC),
        jnp.swapaxes(circ_next, 4, 5),
        height_next.reshape(1, 2, STEPS, COMPS, THICK, ARC),
        patch_load,
    )


def solution(mesh):
    in_specs = (
        P(None, None, "span", "blk"),
        P(None, None, "span", "blk"),
        P(None, "span", "blk"),
        P("blk", None, None, None, None, "span"),
        P("span", None, None, None, None, "blk"),
        P("blk", "span", None),
        P("blk", "span", None),
    )
    out_specs = (
        P(None, None, "span", "blk"),
        P("blk", None, None, None, None, "span"),
        P("span", None, None, None, None, "blk"),
        P(None, ("blk", "span")),
    )
    return jax.shard_map(local, mesh=mesh, in_specs=in_specs, out_specs=out_specs, check_vma=False)
```

```python
import jax
import jax.numpy as jnp
from jax import lax
from jax.experimental import pallas as pl
from jax.experimental.pallas import tpu as pltpu
from jax.sharding import PartitionSpec as P

STEPS = 6
COMPS = 3
THICK = 24
HEIGHT = 16
ARC = 128
FLAT = THICK * HEIGHT
LAYERS = 3
FACE_ROWS = STEPS * COMPS * THICK
PAD_ROWS = 8 * COMPS * THICK
LOAD_ROW = STEPS * COMPS
PATCH_DEV = 32
DEVICES = 128


def roll(values, shift, axis):
    shift %= values.shape[axis]
    return values if shift == 0 else pltpu.roll(values, shift, axis)


def iota(shape, axis):
    return lax.broadcasted_iota(jnp.int32, shape, axis)


def thickness_rows(first, layer, stride=1):
    return pl.ds(first + layer * stride, 8, stride=LAYERS * stride)


def coefficients(modulus, w):
    lane = iota((8, ARC), 1)
    sub = iota((8, ARC), 0)
    zero = jnp.zeros((8, ARC), jnp.float32)
    moduli = [
        roll(modulus[thickness_rows(0, l, HEIGHT), :], 0, 1) for l in range(LAYERS)
    ]
    west = [zero] * LAYERS
    east = [zero] * LAYERS
    for h in range(HEIGHT):
        on_west = lane == h
        on_east = lane == (h - 1) % ARC
        if h + 1 < HEIGHT:
            above = [
                roll(modulus[thickness_rows(h + 1, l, HEIGHT), :], h + 1, 1) for l in range(LAYERS)
            ]
        for l in range(LAYERS):
            m = moduli[l]
            w["along_a"][h, l] = jnp.where(on_east, 0.0, 0.02 * (m + roll(m, -1, 1)))
            if l + 1 < LAYERS:
                w["along_k"][h, l] = 0.02 * (m + moduli[l + 1])
            else:
                w["along_k"][h, l] = jnp.where(sub == 7, 0.0, 0.02 * (m + roll(moduli[0], -1, 0)))
            if h + 1 < HEIGHT:
                w["along_h"][h, l] = 0.02 * (m + roll(above[l], -1, 1))
            imp = jnp.sqrt(m)
            damp = jnp.where(on_west | on_east, imp, 0.0)
            if h == 0:
                damp = damp + imp
                w["faces"][2, l] = 5.0 * imp
            if h == HEIGHT - 1:
                damp = damp + imp
                w["faces"][3, l] = 5.0 * imp
            w["keep"][h, l] = 1.0 - 0.2 * damp
            west[l] = jnp.where(on_west, 5.0 * imp, west[l])
            east[l] = jnp.where(on_east, 5.0 * imp, east[l])
        if h + 1 < HEIGHT:
            moduli = above
    for l in range(LAYERS):
        w["faces"][0, l] = west[l]
        w["faces"][1, l] = east[l]


def load_state(source, scale, kept, used):
    for h in range(HEIGHT):
        for c in range(COMPS):
            for l in range(LAYERS):
                rows = thickness_rows(c * THICK * HEIGHT + h, l, HEIGHT)
                values = source[rows, :]
                if scale != 1.0:
                    values = scale * values
                values = roll(values, h, 1)
                kept[h, c * LAYERS + l] = values
                used[h, c * LAYERS + l] = values


def sides():
    east = lax.axis_index("blk") % 2 == 0
    span = lax.axis_index("span")
    north = span % 2 == 0
    inner = (span > 0) & (span + 1 < lax.axis_size("span"))
    return east, north, inner


def face_rates(w):
    lane = iota((8, ARC), 1)
    zero = jnp.zeros((8, ARC), jnp.float32)

    def rates(c, l):
        b = c * LAYERS + l
        west, east = zero, zero
        for h in range(HEIGHT):
            v = w["vel"][h, b]
            west = jnp.where(lane == h, v, west)
            east = jnp.where(lane == (h - 1) % ARC, v, east)
        north = roll(w["faces"][3, l] * w["vel"][HEIGHT - 1, b], 1 - HEIGHT, 1)
        return w["faces"][0, l] * west, w["faces"][1, l] * east, w["faces"][2, l] * w["vel"][0, b], north

    return rates


def record(step, rates, data, sends, w):
    south_of, north_of = data
    send_first, send_second = sends
    _, to_north, inner = sides()
    weight = jnp.where(inner, 1.0, 0.0)
    for c in range(COMPS):
        for l in range(LAYERS):
            b = c * LAYERS + l
            rate_west, rate_east, rate_south, rate_north = rates(c, l)
            rows = thickness_rows(step * (COMPS * THICK) + c * THICK, l)
            g = w["g_west"][rows, :]
            w["inject"][0, b] = 0.04 * g
            w["send_west"][rows, :] = 2.0 * rate_west - g
            g = w["g_east"][rows, :]
            w["inject"][1, b] = 0.04 * g
            w["send_east"][rows, :] = 2.0 * rate_east - g
            w["load"][b] = w["load"][b] + (g - rate_east)
            g = south_of(rows, step * (COMPS * THICK) + c * THICK, l)
            w["inject"][2, b] = 0.04 * g
            south = 2.0 * rate_south - g
            g = north_of(rows, step * (COMPS * THICK) + c * THICK, l)
            w["inject"][3, b] = roll(0.04 * g, HEIGHT - 1, 1)
            north = 2.0 * rate_north - g
            send_first[rows, :] = jnp.where(to_north, north, south)
            send_second[rows, :] = weight * jnp.where(to_north, south, north)


def injected(h, at, w):
    lane = iota((8, ARC), 1)
    on_west = lane == h
    on_edge = on_west | (lane == (h - 1) % ARC)
    g = jnp.where(on_edge, jnp.where(on_west, w["inject"][0, at], w["inject"][1, at]), 0.0)
    if h == 0:
        g = g + w["inject"][2, at]
    if h == HEIGHT - 1:
        g = g + w["inject"][3, at]
    return g


def update(w, from_cur=None, from_vel=None, sink=None, inject=True):
    from_cur = w["cur"] if from_cur is None else from_cur
    from_vel = w["vel"] if from_vel is None else from_vel
    blocks = [(c, l) for c in range(COMPS) for l in range(LAYERS)]
    cur = {b: from_cur[0, b[0] * LAYERS + b[1]] for b in blocks}
    left = {b: roll(cur[b], -1, 1) for b in blocks}
    rising = {}
    for h in range(HEIGHT):
        last = h + 1 == HEIGHT
        cur_next, left_next = {}, {}
        for c in range(COMPS):
            flux_k = []
            for l in range(LAYERS):
                here = cur[c, l]
                over = cur[c, l + 1] if l + 1 < LAYERS else roll(cur[c, 0], -1, 0)
                flux_k.append(w["along_k"][h, l] * (over - here))
            for l in range(LAYERS):
                b = (c, l)
                at = c * LAYERS + l
                here = cur[b]
                flux_a = w["along_a"][h, l] * (left[b] - here)
                total = flux_k[l] - (flux_k[l - 1] if l else roll(flux_k[LAYERS - 1], 1, 0))
                back = flux_a
                if h:
                    back = back + rising[b]
                total = total + flux_a - roll(back, 1, 1)
                if not last:
                    cur_next[b] = from_cur[h + 1, at]
                    left_next[b] = roll(cur_next[b], -1, 1)
                    rising[b] = w["along_h"][h, l] * (left_next[b] - here)
                    total = total + rising[b]
                if inject:
                    total = total + injected(h, at, w)
                v = w["keep"][h, l] * from_vel[h, at] + total
                if sink is None:
                    w["vel"][h, at] = v
                    w["cur"][h, at] = here + v
                else:
                    sink(h, at, here + v)
        cur, left = cur_next, left_next


def gather_rows(history, offset):
    lane = iota((24, ARC), 1)
    parts = []
    for v in range(3):
        part = None
        for t in range(8):
            rows = roll(history[pl.ds(8 * v + t, 24, stride=THICK), :], HEIGHT * t - offset, 1)
            part = rows if part is None else jnp.where(lane >= HEIGHT * t, rows, part)
        parts.append(part)
    return jnp.concatenate(parts, axis=1)


def scatter_rows(flat, history, offset):
    for v in range(3):
        part = flat[:, v * ARC : (v + 1) * ARC]
        for t in range(8):
            history[pl.ds(8 * v + t, 24, stride=THICK), :] = roll(part, offset - HEIGHT * t, 1)


def split(values):
    high = values.astype(jnp.bfloat16)
    rest = values - high.astype(jnp.float32)
    mid = rest.astype(jnp.bfloat16)
    low = (rest - mid.astype(jnp.float32)).astype(jnp.bfloat16)
    return high, mid, low


def pick(values, one_hot, transposed):
    dims = (((1,), (1 if transposed else 0,)), ((), ()))
    total = None
    for part in split(values):
        term = lax.dot_general(part, one_hot, dims, preferred_element_type=jnp.float32)
        total = term if total is None else total + term
    return total


def pairing(match):
    return jnp.where(iota((FLAT, FLAT), 0) == match[...], 1.0, 0.0).astype(jnp.bfloat16)


def sweep(first_step, data, sends, w):
    def one(step, carry):
        record(step, face_rates(w), data, sends, w)
        update(w)
        return carry

    lax.fori_loop(first_step, STEPS - 1, one, 0)
    record(STEPS - 1, face_rates(w), data, sends, w)


WORK = ("inject", "load", "g_west", "g_east", "send_west", "send_east")
COEFFICIENTS = ("along_a", "along_h", "along_k", "keep", "faces")
BLOCK = (8, ARC)
STATE_SHAPE = (HEIGHT, COMPS * LAYERS) + BLOCK
COEFFICIENT_SHAPES = ((HEIGHT, LAYERS) + BLOCK,) * 4 + ((4, LAYERS) + BLOCK,)
INJECT_SHAPE = (4, COMPS * LAYERS) + BLOCK


def work_shapes():
    shapes = (INJECT_SHAPE, (COMPS * LAYERS,) + BLOCK) + ((PAD_ROWS, ARC),) * 4
    return [pltpu.VMEM(shape, jnp.float32) for shape in shapes]


def clear_tail(w):
    tail = jnp.zeros((PAD_ROWS - FACE_ROWS, ARC), jnp.float32)
    for name in ("send_west", "send_east"):
        w[name][FACE_ROWS:, :] = tail


def spread_guess(circ, side, history, offset):
    rows = STEPS * COMPS * HEIGHT
    unit = jnp.where(iota((THICK, THICK), 0) == iota((THICK, THICK), 1), 1.0, 0.0).astype(jnp.bfloat16)
    total = None
    for part in split(circ[side * rows : (side + 1) * rows, :]):
        term = lax.dot_general(unit, part, (((1,), (1,)), ((), ())), preferred_element_type=jnp.float32)
        total = term if total is None else total + term
    total = jnp.concatenate([total, jnp.zeros((THICK, 3 * ARC - rows), jnp.float32)], axis=1)
    for i in range(STEPS * COMPS):
        tile = total[:, i // 8 * ARC : (i // 8 + 1) * ARC]
        history[i * THICK : (i + 1) * THICK, :] = roll(tile, offset - HEIGHT * (i % 8), 1)


def first_kernel(disp, velocity, modulus, circ, rising, pair_match, patch_owner, *refs):
    first_c, second_c, first_h, second_h, match, owner, cur0, vel0 = refs[:8]
    w = dict(zip(COEFFICIENTS, refs[8:13]))
    disp_in, velocity_in, modulus_in, circ_in, rising_in, sems, w["cur"], w["vel"] = refs[13:21]
    w.update(zip(WORK, refs[21:]))
    copies = [
        pltpu.make_async_copy(source, target, sems.at[i])
        for i, (source, target) in enumerate(
            (
                (modulus, modulus_in),
                (velocity, velocity_in),
                (disp, disp_in),
                (circ, circ_in),
                (rising, rising_in),
                (pair_match, match),
                (patch_owner, owner),
            )
        )
    ]
    for copy in copies:
        copy.start()
    clear_tail(w)
    copies[0].wait()
    coefficients(modulus_in, w)
    copies[1].wait()
    load_state(velocity_in, 0.2, vel0, w["vel"])
    copies[2].wait()
    load_state(disp_in, 1.0, cur0, w["cur"])
    copies[3].wait()
    spread_guess(circ_in, 0, w["g_west"], 0)
    spread_guess(circ_in, 1, w["g_east"], -1)
    for copy in copies[4:]:
        copy.wait()
    data = (
        lambda rows, at, l: rising_in[thickness_rows(at, l), :],
        lambda rows, at, l: rising_in[thickness_rows(FACE_ROWS + at, l), :],
    )
    w["load"][...] = jnp.zeros_like(w["load"])
    sweep(0, data, (first_h, second_h), w)
    west = pick(gather_rows(w["send_west"], 0), pairing(match), True)
    east = gather_rows(w["send_east"], -1)
    to_east, _, _ = sides()
    first_c[...] = jnp.where(to_east, east, west)
    second_c[...] = jnp.where(to_east, west, east)


def middle_kernel(match, cur0, vel0, *refs):
    w = dict(zip(COEFFICIENTS, refs[:5]))
    rates, one_hot, w["cur"], w["vel"] = refs[5:]
    one_hot[...] = pairing(match)
    of = face_rates(w)
    for c in range(COMPS):
        for l in range(LAYERS):
            for side, values in enumerate(of(c, l)):
                rates[side, c * LAYERS + l] = values
    update(w, inject=False)


def second_kernel(got_first_c, got_second_c, got_first_h, got_second_h, pairs, rates, owner, cur1, vel1, *refs):
    w = dict(zip(COEFFICIENTS, refs[:5]))
    first_c, second_c, first_h, second_h, shares, inject, w["cur"], w["vel"] = refs[5:13]
    w.update(zip(WORK, (inject,) + refs[13:]))
    clear_tail(w)
    one_hot = pairs[...]
    to_east, to_north, _ = sides()
    first, second = got_first_c[...], got_second_c[...]
    scatter_rows(pick(jnp.where(to_east, second, first), one_hot, False), w["g_west"], 0)
    scatter_rows(jnp.where(to_east, first, second), w["g_east"], -1)
    data = (
        lambda rows, at, l: jnp.where(to_north, got_second_h[rows, :], got_first_h[rows, :]),
        lambda rows, at, l: jnp.where(to_north, got_first_h[rows, :], got_second_h[rows, :]),
    )
    w["load"][...] = jnp.zeros_like(w["load"])
    record(0, lambda c, l: [rates[side, c * LAYERS + l] for side in range(4)], data, (first_h, second_h), w)
    for h in range(HEIGHT):
        for at in range(COMPS * LAYERS):
            g = injected(h, at, w)
            w["vel"][h, at] = w["vel"][h, at] + g
            w["cur"][h, at] = w["cur"][h, at] + g
    sweep(1, data, (first_h, second_h), w)
    for c in range(COMPS):
        for l in range(LAYERS):
            w["send_east"][thickness_rows(FACE_ROWS + c * THICK, l), :] = w["load"][c * LAYERS + l]
    west = pick(gather_rows(w["send_west"], 0), one_hot, True)
    east = gather_rows(w["send_east"], -1)
    first_c[...] = jnp.where(to_east, east, west)
    second_c[...] = jnp.where(to_east, west, east)
    owners = owner[...]
    device = owners // PATCH_DEV
    spot = owners - device * PATCH_DEV
    holder = jnp.where(iota((DEVICES, FLAT), 0) == device, 1.0, 0.0).astype(jnp.bfloat16)
    at = iota((PATCH_DEV, FLAT), 0) == spot
    terms = [
        jnp.where(at, east[LOAD_ROW + c : LOAD_ROW + c + 1, :], 0.0) for c in range(COMPS)
    ]
    terms.append(jnp.zeros((PATCH_DEV, FLAT), jnp.float32))
    total = None
    for part in split(jnp.concatenate(terms, axis=0)):
        term = lax.dot_general(holder, part, (((1,), (1,)), ((), ())), preferred_element_type=jnp.float32)
        total = term if total is None else total + term
    shares[...] = total


def end_kernel(cur, vel, inject, *refs):
    w = dict(zip(COEFFICIENTS, refs[:5]))
    disp_end, ending = refs[5:]
    w["inject"] = inject

    def keep_end(h, at, values):
        ending[h, at] = values

    update(w, cur, vel, keep_end)
    for h in range(HEIGHT):
        for c in range(COMPS):
            for l in range(LAYERS):
                rows = thickness_rows(c * THICK * HEIGHT + h, l, HEIGHT)
                disp_end[rows, :] = roll(ending[h, c * LAYERS + l], -h, 1)


def face_kernel(got_first_c, got_second_c, got_first_h, got_second_h, match, _, *refs):
    circ_next, height_next, turned_rows, sems = refs
    to_east, to_north, _ = sides()
    first_at = pl.multiple_of(jnp.where(to_north, FACE_ROWS, 0), 8)
    second_at = pl.multiple_of(jnp.where(to_north, 0, FACE_ROWS), 8)
    copies = [
        pltpu.make_async_copy(got_first_h, height_next.at[pl.ds(first_at, FACE_ROWS)], sems.at[0]),
        pltpu.make_async_copy(got_second_h, height_next.at[pl.ds(second_at, FACE_ROWS)], sems.at[1]),
    ]
    for copy in copies:
        copy.start()
    first, second = got_first_c[...], got_second_c[...]
    west = pick(jnp.where(to_east, second, first), pairing(match), False)
    east = jnp.where(to_east, first, second)
    lanes = 32 * HEIGHT
    spot = iota((FLAT, lanes), 1)
    k, h = spot % 32, spot // 32
    turn = jnp.where((iota((FLAT, lanes), 0) == k * HEIGHT + h) & (k < THICK), 1.0, 0.0).astype(jnp.bfloat16)
    turned = pick(jnp.concatenate([west, east], axis=0), turn, False)
    face = STEPS * COMPS * HEIGHT
    for side in range(2):
        part = turned[24 * side : 24 * (side + 1), :]
        for h in range(HEIGHT):
            tile = part[:, h // 4 * ARC : (h // 4 + 1) * ARC]
            turned_rows[pl.ds(24 * HEIGHT * side + h, 24, stride=HEIGHT), :] = roll(tile, -32 * (h % 4), 1)
        first_row = 24 * HEIGHT * side
        circ_next[face * side : face * (side + 1), :] = turned_rows[first_row : first_row + face, 0:THICK]
    for copy in copies:
        copy.wait()


def sum_kernel(shares, _, patch_load):
    total = jnp.sum(shares[...], axis=0, keepdims=True)
    for c in range(COMPS):
        patch_load[c : c + 1, :] = total[:, c * PATCH_DEV : (c + 1) * PATCH_DEV]


def held(*arrays):
    def kernel(*refs):
        pass

    count = len(arrays)
    return pl.pallas_call(
        kernel,
        out_shape=tuple(f32(*a.shape) for a in arrays),
        in_specs=[VMEM] * count,
        out_specs=(VMEM,) * count,
        input_output_aliases={i: i for i in range(count)},
        compiler_params=PARAMS,
        cost_estimate=pl.CostEstimate(flops=4 * 10**6, bytes_accessed=4 * 10**6, transcendentals=0),
    )(*arrays)


def f32(*shape):
    return jax.ShapeDtypeStruct(shape, jnp.float32)


PARAMS = pltpu.CompilerParams(vmem_limit_bytes=24 * 1024 * 1024)
VMEM = pl.BlockSpec(memory_space=pltpu.VMEM)
ANY = pl.BlockSpec(memory_space=pl.ANY)
HBM = pl.BlockSpec(memory_space=pltpu.HBM)


def exchanged(first_c, second_c, first_h, second_h):
    blks, spans = lax.axis_size("blk"), lax.axis_size("span")

    def pairs(count, start):
        return [p for i in range(start, count, 2) for p in ((i, (i + 1) % count), ((i + 1) % count, i))]

    first_h = lax.ppermute(first_h, "span", pairs(spans, 0))
    second_h = lax.ppermute(second_h, "span", pairs(spans, 1))
    first_c = lax.ppermute(first_c, "blk", pairs(blks, 0))
    second_c = lax.ppermute(second_c, "blk", pairs(blks, 1))
    return first_c, second_c, first_h, second_h


def local(disp, velocity, modulus, guess_circ, guess_height, pair_match, patch_owner):
    disp = disp.reshape(COMPS * FLAT, ARC)
    velocity = velocity.reshape(COMPS * FLAT, ARC)
    modulus = modulus.reshape(FLAT, ARC)
    side_rows = STEPS * COMPS * HEIGHT
    circ = jnp.swapaxes(guess_circ, 4, 5).reshape(2 * side_rows, THICK)
    rising = guess_height.reshape(2 * FACE_ROWS, ARC)
    match = pair_match.reshape(1, FLAT)
    owner = patch_owner.reshape(1, FLAT)
    face = f32(FACE_ROWS, ARC)
    flat = f32(24, FLAT)
    state = f32(*STATE_SHAPE)
    copied = ((COMPS * FLAT, ARC), (COMPS * FLAT, ARC), (FLAT, ARC), (2 * side_rows, THICK), (2 * FACE_ROWS, ARC))
    row = jax.ShapeDtypeStruct((1, FLAT), jnp.int32)
    inputs = (disp, velocity, modulus, circ, rising, match, owner)
    *sends, match, owner, cur, vel, k1, k2, k3, k4, k5 = pl.pallas_call(
        first_kernel,
        out_shape=(flat, flat, face, face, row, row, state, state) + tuple(f32(*shape) for shape in COEFFICIENT_SHAPES),
        in_specs=[HBM] * 7,
        out_specs=(VMEM,) * 13,
        scratch_shapes=[pltpu.VMEM(shape, jnp.float32) for shape in copied]
        + [pltpu.SemaphoreType.DMA((7,))]
        + [pltpu.VMEM(STATE_SHAPE, jnp.float32)] * 2
        + work_shapes(),
        compiler_params=PARAMS,
    )(*(pltpu.with_memory_space_constraint(x, pltpu.HBM) for x in inputs))
    coefficient = (k1, k2, k3, k4, k5)
    first_c, second_c, first_h, second_h = exchanged(*sends)
    for _ in range(1):
        (second_c,) = held(second_c)
    got = first_c, second_c, first_h, second_h
    rates, pairs, cur, vel = pl.pallas_call(
        middle_kernel,
        out_shape=(f32(*INJECT_SHAPE), jax.ShapeDtypeStruct((FLAT, FLAT), jnp.bfloat16), state, state),
        in_specs=[VMEM] * 8,
        out_specs=(VMEM,) * 4,
        input_output_aliases={1: 2, 2: 3},
        compiler_params=PARAMS,
        cost_estimate=pl.CostEstimate(flops=3 * 10**6, bytes_accessed=4 * 10**6, transcendentals=0),
    )(match, cur, vel, *coefficient)
    *sends, shares, inject, cur, vel = pl.pallas_call(
        second_kernel,
        out_shape=(flat, flat, face, face, f32(DEVICES, ARC), f32(*INJECT_SHAPE), state, state),
        in_specs=[VMEM] * 14,
        out_specs=(VMEM,) * 8,
        scratch_shapes=work_shapes()[1:],
        input_output_aliases={7: 6, 8: 7},
        compiler_params=PARAMS,
    )(*got, pairs, rates, owner, cur, vel, *coefficient)
    got = exchanged(*sends)
    shares = lax.all_to_all(shares, ("blk", "span"), split_axis=0, concat_axis=0, tiled=True)
    disp_end = pl.pallas_call(
        end_kernel,
        out_shape=f32(COMPS * FLAT, ARC),
        in_specs=[VMEM] * 8,
        out_specs=VMEM,
        scratch_shapes=[pltpu.VMEM(STATE_SHAPE, jnp.float32)],
        compiler_params=PARAMS,
    )(cur, vel, inject, *coefficient)
    circ_next, height_next = pl.pallas_call(
        face_kernel,
        out_shape=(f32(2 * side_rows, THICK), f32(2 * FACE_ROWS, ARC)),
        in_specs=[VMEM, VMEM, ANY, ANY, VMEM, ANY],
        out_specs=(VMEM, ANY),
        scratch_shapes=[pltpu.VMEM((2 * 24 * HEIGHT, ARC), jnp.float32), pltpu.SemaphoreType.DMA((2,))],
        compiler_params=PARAMS,
    )(*got, match, pltpu.with_memory_space_constraint(disp_end, pltpu.HBM))
    patch_load = pl.pallas_call(
        sum_kernel, out_shape=f32(COMPS, PATCH_DEV), in_specs=[VMEM, ANY], out_specs=VMEM, compiler_params=PARAMS
    )(shares, pltpu.with_memory_space_constraint(circ_next, pltpu.HBM))
    circ_next = circ_next.reshape(1, 2, STEPS, COMPS, HEIGHT, THICK)
    return (
        disp_end.reshape(COMPS, THICK, HEIGHT, ARC),
        jnp.swapaxes(circ_next, 4, 5),
        height_next.reshape(1, 2, STEPS, COMPS, THICK, ARC),
        patch_load,
    )


def solution(mesh):
    in_specs = (
        P(None, None, "span", "blk"),
        P(None, None, "span", "blk"),
        P(None, "span", "blk"),
        P("blk", None, None, None, None, "span"),
        P("span", None, None, None, None, "blk"),
        P("blk", "span", None),
        P("blk", "span", None),
    )
    out_specs = (
        P(None, None, "span", "blk"),
        P("blk", None, None, None, None, "span"),
        P("span", None, None, None, None, "blk"),
        P(None, ("blk", "span")),
    )
    return jax.shard_map(local, mesh=mesh, in_specs=in_specs, out_specs=out_specs, check_vma=False)
```
